32 devices in a mesh: row: 8 (over z, core), col: 4 (over y, x).
Axes of the slice: x: 2, y: 2, z: 4, core: 2. Of those that a mesh axis runs over, the one named last changes fastest.
Arguments:
- out_grad: bfloat16 [16384, 256], P(('row', 'col')), may hold values from -6 to 6
- out_bits: int32 [16384, 16], P(('row', 'col')), may hold values from 0 to 65535
- agg_saved: bfloat16 [16384, 256], P(('row', 'col')), may hold values from -6 to 6
- weight: bfloat16 [256, 256], replicated, may hold values from -0.375 to 0.375
- tiles: bfloat16 [8, 4, 512, 128, 128], P('row', 'col'), may hold values from -0.0625 to 0.0625
- tile_coords: int32 [8, 4, 512, 2], P('row', 'col'), may hold values from 0 to 31, as said below
- tile_count: int32 [8, 4], P('row', 'col'), may hold values from 64 to 512, as said below
- in_bits: int32 [16384, 16], P(('row', 'col')), may hold values from 0 to 65535
Outputs:
- weight_grad: float32 [256, 256], replicated
- prev_grad: bfloat16 [16384, 256], P(('row', 'col'))
The draws below stay inside these ranges and needn't reach their ends.
Inputs may be any that keep to these rules, and one draw needn't show every extreme that they name: `tile_coords`: within one block, all 512 slots name distinct tile positions; tile rows are below 16 and tile columns below 32. `tile_count`: slots at or beyond a block's count are ignored; some block uses all 512 slots.
All inputs are finite; a program needn't handle non-finite values.
Results may differ from the reference program's by a relative error of at most 0.0049.
Values may be sent and summed in bfloat16 or wider, within the bound.
A program may use at most 128 MiB of HBM per device.

```python
import jax
import jax.numpy as jnp
from jax import lax

H = 256
TILE = 128
CH = 512
MAXT = 512
NODES = 16384
N_ROW = 8
N_COL = 4


def draw_tile_coords(key, part):
    tile_rows = N_COL * CH // TILE
    tile_cols = N_ROW * CH // TILE
    device_keys = jax.random.split(key, N_ROW * N_COL)

    def one_device(device_key):
        order = jax.random.permutation(device_key, tile_rows * tile_cols)[:MAXT]
        return jnp.stack([order // tile_cols, order % tile_cols], axis=-1)
    return jax.vmap(one_device)(device_keys).reshape(N_ROW, N_COL, MAXT, 2).astype(jnp.int32)


def draw_tile_count(key, part):
    lowest = MAXT // 8
    spread = MAXT - lowest + 1
    first_draw = jax.random.randint(jax.random.fold_in(key, 11), (N_ROW * N_COL,), 0, spread)
    second_draw = jax.random.randint(jax.random.fold_in(key, 12), (N_ROW * N_COL,), 0, spread)
    counts = lowest + first_draw * second_draw // max(spread - 1, 1)
    chosen = jax.random.randint(jax.random.fold_in(key, 13), (), 0, N_ROW * N_COL)
    positions = jnp.arange(N_ROW * N_COL, dtype=jnp.int32)
    counts = jnp.where(positions == chosen, MAXT, counts)
    return counts.reshape(N_ROW, N_COL).astype(jnp.int32)


def with_ends(array, key, least, high):
    dims = array.shape
    place = [jax.random.randint(jax.random.fold_in(key, axis), (), 0, dims[axis]) for axis in range(len(dims))]
    array = array.at[tuple(place)].set(least)
    longest = dims.index(max(dims))
    place[longest] = (place[longest] + 1) % dims[longest]
    return array.at[tuple(place)].set(high)


def shard_levels(own_key, dims, shards, least, largest):
    gain, own = 1.0, jax.random.fold_in(own_key, 6)
    for dim, shards_of in shards:
        steps = jnp.exp(jax.random.uniform(jax.random.fold_in(own, dim), (shards_of,), jnp.float32, least / len(shards), largest / len(shards)))
        gain = gain * jnp.repeat(steps, dims[dim] // shards_of).reshape([-1 if axis == dim else 1 for axis in range(len(dims))])
    return gain


def centred(key, extent, deviation, bound, shards=(), kind=jnp.bfloat16):
    gain = shard_levels(key, extent, shards, -0.22, 0.18) if shards else 1.0
    entries = jax.random.normal(key, extent, jnp.float32) * deviation * gain
    return jnp.minimum(jnp.maximum(entries, -bound), bound).astype(kind)


def setup_inputs(seed: int = 0) -> dict:
    key_list = jax.random.split(jax.random.key(seed), 9)
    out_grad = centred(key_list[0], (NODES, H), 1.0, 6.0, ((0, 32),))
    out_bits = with_ends(jax.random.randint(key_list[1], (NODES, H // 16), 0, 65536), jax.random.fold_in(key_list[1], 1), 0, 65535).astype(jnp.int32)
    agg_saved = centred(key_list[2], (NODES, H), 1.0, 6.0, ((0, 32),))
    weight = centred(key_list[3], (H, H), H ** -0.5, 0.375)
    tiles = centred(key_list[4], (N_ROW, N_COL, MAXT, TILE, TILE), (MAXT * TILE * TILE // (2 * CH)) ** -0.5, 0.0625, ((0, 8), (1, 4)))
    tile_coords = draw_tile_coords(jax.random.fold_in(key_list[8], 71), 0)
    tile_count = draw_tile_count(jax.random.fold_in(key_list[8], 71), 0)
    in_bits = with_ends(jax.random.randint(key_list[7], (NODES, H // 16), 0, 65536), jax.random.fold_in(key_list[7], 1), 0, 65535).astype(jnp.int32)
    return {"out_grad": out_grad, "out_bits": out_bits, "agg_saved": agg_saved, "weight": weight, "tiles": tiles, "tile_coords": tile_coords, "tile_count": tile_count, "in_bits": in_bits}


def unpack(packed):
    shift_list = jnp.arange(16, dtype=jnp.int32)
    bit_values = jnp.right_shift(packed[:, :, None], shift_list[None, None, :]) & 1
    return bit_values.reshape(packed.shape[0], packed.shape[1] * 16)


def block_product(block_tiles, block_coords, tile_total, row_values):
    tile_rows = row_values.reshape(-1, TILE, H)
    picked = tile_rows[block_coords[:, 0]].astype(jnp.float32)
    products = jnp.einsum('kij,kih->kjh', block_tiles.astype(jnp.float32), picked)
    alive_mask = jnp.arange(MAXT, dtype=jnp.int32) < tile_total
    products = jnp.where(alive_mask[:, None, None], products, jnp.zeros_like(products))
    col_tiles = N_ROW * CH // TILE
    sums = jnp.zeros((col_tiles, TILE, H), jnp.float32).at[block_coords[:, 1]].add(products)
    return sums.reshape(col_tiles * TILE, H)


def reference(out_grad, out_bits, agg_saved, weight, tiles, tile_coords, tile_count, in_bits):
    masked_grad = jnp.where(unpack(out_bits) == 1, out_grad, jnp.zeros_like(out_grad))
    weight_grad = lax.dot_general(agg_saved, masked_grad, (((0,), (0,)), ((), ())),
                                  preferred_element_type=jnp.float32) * (NODES ** -0.5)
    hidden_grad = lax.dot_general(masked_grad, weight, (((1,), (1,)), ((), ())),
                                  preferred_element_type=jnp.float32).astype(jnp.bfloat16)
    row_blocks = hidden_grad.reshape(N_ROW, N_COL * CH, H)

    def accumulate(running, row_index):
        def one_block(col_index):
            return block_product(tiles[row_index, col_index], tile_coords[row_index, col_index],
                                 tile_count[row_index, col_index], row_blocks[row_index])
        block_sums = lax.map(one_block, jnp.arange(N_COL, dtype=jnp.int32))
        block_sums = block_sums.reshape(N_COL, N_ROW, CH, H).transpose(1, 0, 2, 3)
        return running + block_sums, None

    running, unused = lax.scan(accumulate, jnp.zeros((N_ROW, N_COL, CH, H), jnp.float32),
                               jnp.arange(N_ROW, dtype=jnp.int32))
    node_grad = running.reshape(NODES, H)
    prev_grad = jnp.where(unpack(in_bits) == 1, node_grad, jnp.zeros_like(node_grad)).astype(jnp.bfloat16)
    return weight_grad, prev_grad
```

```python
import functools
import math

import jax
import jax.numpy as jnp
from jax import lax
from jax.experimental import pallas as pl
from jax.experimental.pallas import tpu as pltpu
from jax.sharding import PartitionSpec as P

TILE = 128
PAIR = 2 * TILE
PARTS = 2
MESH = pl.DeviceIdType.MESH
F32 = jnp.float32
BF16 = jnp.bfloat16


def bit_mask(bits, features):
    words = bits.shape[1]
    low = (bits & 255).astype(F32).astype(BF16)
    high = ((bits >> 8) & 255).astype(F32).astype(BF16)
    feature = lax.broadcasted_iota(jnp.int32, (words, features), 1)
    word = lax.broadcasted_iota(jnp.int32, (words, features), 0)
    own = (feature >> 4) == word
    in_low = (feature & 15) < 8
    pick_low = jnp.where(own & in_low, 1.0, 0.0).astype(BF16)
    pick_high = jnp.where(own & ~in_low, 1.0, 0.0).astype(BF16)
    byte = jnp.dot(low, pick_low, preferred_element_type=F32)
    byte += jnp.dot(high, pick_high, preferred_element_type=F32)
    shift = lax.broadcasted_iota(jnp.int32, (bits.shape[0], features), 1) & 7
    return (byte.astype(jnp.int32) >> shift) & 1


def prepare(scale, grad_ref, bits_ref, agg_ref, weight_ref, part_ref, hidden_ref):
    mask = bit_mask(bits_ref[...], grad_ref.shape[1])
    masked = jnp.where(mask == 1, grad_ref[...].astype(F32), 0.0).astype(BF16)
    hidden_ref[...] = lax.dot_general(
        weight_ref[...], masked, (((1,), (1,)), ((), ())), preferred_element_type=F32
    ).astype(BF16)
    part_ref[...] = scale * lax.dot_general(
        agg_ref[...], masked, (((0,), (0,)), ((), ())), preferred_element_type=F32
    )


def flip_bits(index, bits, total):
    result = index
    step = 1
    while step < total:
        if bits & step:
            result = result + step * (1 - 2 * ((index // step) % 2))
        step *= 2
    return result


def exchange(
    rows, cols, hidden_ref, part_ref, tiles_ref, table_ref, bits_ref, out_ref, weight_ref,
    tile_buf, gathered, acc, pair_out, pair_in, chain_out, chain_in, mask_buf,
    by_col, col_sum, by_row, row_sum, col_total, total_buf,
    w1_send, w1_recv, w2_send, w2_recv, w3_send, w3_recv, w4_send, w4_recv,
    tile_sem, hid_send, hid_recv, pair_send, pair_recv, chain_send, chain_recv,
):
    slots = tiles_ref.shape[0]
    features, nodes = hidden_ref.shape
    row_tiles = nodes // TILE
    col_tiles = rows * nodes // TILE
    pairs_per = nodes // PAIR
    part = features // PARTS
    chips = rows // 2
    my_row = lax.axis_index("row")
    my_col = lax.axis_index("col")
    place = my_row // 2
    core = my_row % 2
    partner = place * 2 + 1 - core

    loads = []
    chunk = slots // 8
    for piece in range(8):
        span = pl.ds(piece * chunk, chunk)
        load = pltpu.make_async_copy(tiles_ref.at[span], tile_buf.at[span], tile_sem.at[piece])
        load.start()
        loads.append(load)

    barrier = pltpu.get_barrier_semaphore()
    peers = [flip_bits(my_col, k, cols) for k in range(cols)]
    for k in range(1, cols):
        pl.semaphore_signal(barrier, inc=1, device_id=(my_row, peers[k]), device_id_type=MESH)
    mates = [(my_row + i) % rows for i in range(rows)]
    for i in range(1, rows):
        pl.semaphore_signal(barrier, inc=1, device_id=(mates[i], my_col), device_id_type=MESH)
    pl.semaphore_wait(barrier, rows + cols - 2)

    sends = []
    for k in range(1, cols):
        copy = pltpu.make_async_remote_copy(
            src_ref=hidden_ref, dst_ref=gathered.at[my_col],
            send_sem=hid_send.at[k], recv_sem=hid_recv.at[my_col],
            device_id=(my_row, peers[k]), device_id_type=MESH,
        )
        copy.start()
        sends.append(copy)

    gathered[my_col] = hidden_ref[...]
    tile_buf[slots] = jnp.zeros((TILE, TILE), BF16)
    mask_buf[...] = bit_mask(bits_ref[...], features).astype(F32)
    for load in loads:
        load.wait()

    def product(source, pair):
        strips = []
        for i in range(row_tiles):
            base = (source * row_tiles + i) * col_tiles + 2 * pair
            strips.append(jnp.concatenate([tile_buf[table_ref[base]], tile_buf[table_ref[base + 1]]], axis=1))
        return jnp.dot(gathered[source], jnp.concatenate(strips, axis=0), preferred_element_type=F32)

    def hid_wait(k):
        pltpu.make_async_remote_copy(
            src_ref=hidden_ref, dst_ref=gathered.at[peers[k]],
            send_sem=hid_send.at[k], recv_sem=hid_recv.at[peers[k]],
            device_id=(my_row, peers[k]), device_id_type=MESH,
        ).wait_recv()

    for k in range(cols - 1):
        if k:
            hid_wait(k)

        @pl.loop(0, col_tiles // 2)
        def _(pair, k=k):
            value = product(peers[k], pair)
            if k:
                value += acc[pair]
            acc[pair] = value

    hid_wait(cols - 1)

    band = features // cols
    owners = min(rows, band // 8)
    strip = band // owners

    def w1_copy(k):
        return pltpu.make_async_remote_copy(
            src_ref=part_ref.at[pl.ds(pl.multiple_of(peers[k] * band, 8), band)], dst_ref=by_col.at[my_col],
            send_sem=w1_send.at[k], recv_sem=w1_recv.at[my_col],
            device_id=(my_row, peers[k]), device_id_type=MESH,
        )

    def w2_copy(i):
        return pltpu.make_async_remote_copy(
            src_ref=col_sum.at[pl.ds(pl.multiple_of(mates[i] * strip, 8), strip)], dst_ref=by_row.at[my_row],
            send_sem=w2_send.at[i], recv_sem=w2_recv.at[my_row],
            device_id=(mates[i], my_col), device_id_type=MESH,
        )

    def w3_copy(i):
        return pltpu.make_async_remote_copy(
            src_ref=row_sum, dst_ref=col_total.at[pl.ds(pl.multiple_of(my_row * strip, 8), strip)],
            send_sem=w3_send.at[i], recv_sem=w3_recv.at[my_row],
            device_id=(mates[i], my_col), device_id_type=MESH,
        )

    def w4_copy(k):
        return pltpu.make_async_remote_copy(
            src_ref=col_total, dst_ref=total_buf.at[pl.ds(pl.multiple_of(my_col * band, 8), band)],
            send_sem=w4_send.at[k], recv_sem=w4_recv.at[my_col],
            device_id=(my_row, peers[k]), device_id_type=MESH,
        )

    def landed(ref, sem):
        pltpu.make_async_copy(ref, ref, sem).wait()

    def weight_one():
        for k in range(1, cols):
            w1_copy(k).start()

    def weight_two():
        total = part_ref[pl.ds(pl.multiple_of(my_col * band, 8), band), :]
        for k in range(1, cols):
            landed(by_col.at[peers[k]], w1_recv.at[peers[k]])
            total += by_col[peers[k]]
        col_sum[...] = total
        for i in range(1, rows):
            @pl.when(mates[i] < owners)
            def _():
                w2_copy(i).start()

    def weight_three():
        @pl.when(my_row < owners)
        def _():
            mine = pl.ds(pl.multiple_of(my_row * strip, 8), strip)
            total = col_sum[mine, :]
            for i in range(1, rows):
                landed(by_row.at[mates[i]], w2_recv.at[mates[i]])
                total += by_row[mates[i]]
            row_sum[...] = total
            col_total[mine, :] = total
            for i in range(1, rows):
                w3_copy(i).start()

    def weight_four():
        for i in range(1, rows):
            @pl.when(mates[i] < owners)
            def _():
                landed(col_total.at[pl.ds(pl.multiple_of(mates[i] * strip, 8), strip)], w3_recv.at[mates[i]])
        total_buf[pl.ds(pl.multiple_of(my_col * band, 8), band), :] = col_total[...]
        for k in range(1, cols):
            w4_copy(k).start()

    def weight_end():
        for k in range(1, cols):
            landed(total_buf.at[pl.ds(pl.multiple_of(peers[k] * band, 8), band)], w4_recv.at[peers[k]])
        weight_ref[...] = total_buf[...]
        for k in range(1, cols):
            w1_copy(k).wait_send()
            w4_copy(k).wait_send()
        for i in range(1, rows):
            @pl.when(mates[i] < owners)
            def _():
                w2_copy(i).wait_send()

            @pl.when(my_row < owners)
            def _():
                w3_copy(i).wait_send()

    weight_one()

    order = []
    for d in range((chips + 1) // 2):
        order += [chips - 1 - d] + ([d] if d != chips - 1 - d else [])

    def finish(owner):
        for j in range(pairs_per):
            pair = owner * pairs_per + j
            yield j, acc[pair] + product(peers[cols - 1], pair)

    def pair_copy(spot):
        return pltpu.make_async_remote_copy(
            src_ref=pair_out.at[spot], dst_ref=pair_in.at[spot],
            send_sem=pair_send.at[spot], recv_sem=pair_recv.at[spot],
            device_id=(partner, my_col), device_id_type=MESH,
        )

    for spot in order:
        for j, value in finish(2 * spot + 1 - core):
            pair_out[spot, :, pl.ds(j * PAIR, PAIR)] = value.astype(BF16)
        pair_copy(spot).start()
    for spot in order:
        for j, value in finish(2 * spot + core):
            acc[(2 * spot + core) * pairs_per + j] = value

    def chain_copy(way, spot, p):
        return pltpu.make_async_remote_copy(
            src_ref=chain_out.at[way, spot, p], dst_ref=chain_in.at[way, spot, p],
            send_sem=chain_send.at[way, spot, p], recv_sem=chain_recv.at[way, spot, p],
            device_id=(my_row + 2 - 4 * way, my_col), device_id_type=MESH,
        )

    def local_sum(spot, p):
        first = (2 * spot + core) * pairs_per
        own = jnp.concatenate(
            [acc[first + j, p * part:(p + 1) * part, :] for j in range(pairs_per)], axis=1
        )
        return own + pair_in[spot, p * part:(p + 1) * part, :].astype(F32)

    def hop(way, d):
        spot = (1 - way) * (chips - 1 - d) + way * d
        ahead = (1 - 2 * way) * (spot - place)
        behind = (1 - way) * place + way * (chips - 1 - place)

        @pl.when(ahead > 0)
        def _():
            for p in range(PARTS):
                @pl.when(behind > 0)
                def _():
                    chain_copy(way, spot, p).wait_recv()
                    total = local_sum(spot, p) + chain_in[way, spot, p].astype(F32)
                    chain_out[way, spot, p] = total.astype(BF16)

                @pl.when(behind == 0)
                def _():
                    chain_out[way, spot, p] = local_sum(spot, p).astype(BF16)

                chain_copy(way, spot, p).start()

    way = place // ((chips + 1) // 2)
    for spot in order:
        pair_copy(spot).wait_recv()
    weight_two()
    for d in range(chips - 1):
        hop(way, d)
        if d == 0:
            weight_three()
        hop(1 - way, d)
        if d == 0:
            weight_four()

    for p in range(PARTS):
        rows_p = pl.ds(p * part, part)
        first = (2 * place + core) * pairs_per
        for j in range(pairs_per):
            acc[first + j, rows_p, :] += pair_in[place, rows_p, pl.ds(j * PAIR, PAIR)].astype(F32)

        @pl.when(place > 0)
        def _():
            chain_copy(0, place, p).wait_recv()
            for j in range(pairs_per):
                acc[first + j, rows_p, :] += chain_in[0, place, p, :, pl.ds(j * PAIR, PAIR)].astype(F32)

        @pl.when(place < chips - 1)
        def _():
            chain_copy(1, place, p).wait_recv()
            for j in range(pairs_per):
                acc[first + j, rows_p, :] += chain_in[1, place, p, :, pl.ds(j * PAIR, PAIR)].astype(F32)

        for j in range(pairs_per):
            area = (pl.ds(j * PAIR, PAIR), rows_p)
            out_ref[area] = jnp.where(mask_buf[area] > 0.5, acc[first + j, rows_p, :].T, 0.0).astype(BF16)

    weight_end()
    for copy in sends:
        copy.wait_send()
    for spot in order:
        pair_copy(spot).wait_send()
    for spot in range(chips):
        for p in range(PARTS):
            @pl.when(spot > place)
            def _():
                chain_copy(0, spot, p).wait_send()

            @pl.when(spot < place)
            def _():
                chain_copy(1, spot, p).wait_send()


def shards(out_grad, out_bits, agg_saved, weight, tiles, tile_coords, tile_count, in_bits):
    rows = lax.axis_size("row")
    cols = lax.axis_size("col")
    nodes, features = out_grad.shape
    scale = 1.0 / math.sqrt(nodes * rows * cols)
    slots = tiles.shape[2]
    row_tiles = cols * nodes // TILE
    col_tiles = rows * nodes // TILE
    chips = rows // 2
    part = features // PARTS
    vmem = pl.BlockSpec(memory_space=pltpu.VMEM)

    weight_part, hidden = pl.pallas_call(
        functools.partial(prepare, scale),
        out_shape=(
            jax.ShapeDtypeStruct((features, features), F32),
            jax.ShapeDtypeStruct((features, nodes), BF16),
        ),
        in_specs=[vmem] * 4,
        out_specs=(vmem, vmem),
        compiler_params=pltpu.CompilerParams(vmem_limit_bytes=32 * 2**20),
        name="prepare",
    )(out_grad, out_bits, agg_saved, weight)

    spot = tile_coords[0, 0, :, 0] * col_tiles + tile_coords[0, 0, :, 1]
    slot = jnp.arange(slots, dtype=jnp.int32)
    spot = jnp.where(slot < tile_count[0, 0], spot, -1)
    hit = spot[:, None] == jnp.arange(row_tiles * col_tiles, dtype=jnp.int32)[None, :]
    table = jnp.min(jnp.where(hit, slot[:, None], slots), axis=0)

    dma = pltpu.SemaphoreType.DMA
    band = features // cols
    strip = band // min(rows, band // 8)
    prev_grad, weight_grad = pl.pallas_call(
        functools.partial(exchange, rows, cols),
        out_shape=(
            jax.ShapeDtypeStruct((nodes, features), BF16),
            jax.ShapeDtypeStruct((features, features), F32),
        ),
        in_specs=[vmem, vmem, pl.BlockSpec(memory_space=pl.ANY), pl.BlockSpec(memory_space=pltpu.SMEM), vmem],
        out_specs=(vmem, vmem),
        scratch_shapes=[
            pltpu.VMEM((slots + 1, TILE, TILE), BF16),
            pltpu.VMEM((cols, features, nodes), BF16),
            pltpu.VMEM((col_tiles // 2, features, PAIR), F32),
            pltpu.VMEM((chips, features, nodes), BF16),
            pltpu.VMEM((chips, features, nodes), BF16),
            pltpu.VMEM((2, chips, PARTS, part, nodes), BF16),
            pltpu.VMEM((2, chips, PARTS, part, nodes), BF16),
            pltpu.VMEM((nodes, features), F32),
            pltpu.VMEM((cols, band, features), F32),
            pltpu.VMEM((band, features), F32),
            pltpu.VMEM((rows, strip, features), F32),
            pltpu.VMEM((strip, features), F32),
            pltpu.VMEM((band, features), F32),
            pltpu.VMEM((features, features), F32),
            dma((cols,)),
            dma((cols,)),
            dma((rows,)),
            dma((rows,)),
            dma((rows,)),
            dma((rows,)),
            dma((cols,)),
            dma((cols,)),
            dma((8,)),
            dma((cols,)),
            dma((cols,)),
            dma((chips,)),
            dma((chips,)),
            dma((2, chips, PARTS)),
            dma((2, chips, PARTS)),
        ],
        compiler_params=pltpu.CompilerParams(
            collective_id=0, has_side_effects=True, vmem_limit_bytes=56 * 2**20
        ),
        cost_estimate=pl.CostEstimate(
            flops=2 * row_tiles * col_tiles * TILE * TILE * features,
            bytes_accessed=slots * TILE * TILE * 2, transcendentals=0,
        ),
        name="exchange",
    )(hidden, weight_part, tiles[0, 0], table, in_bits)
    return weight_grad, prev_grad


def solution(mesh):
    return jax.shard_map(
        shards,
        mesh=mesh,
        in_specs=(
            P(("row", "col"), None),
            P(("row", "col"), None),
            P(("row", "col"), None),
            P(),
            P("row", "col", None, None, None),
            P("row", "col", None, None),
            P("row", "col"),
            P(("row", "col"), None),
        ),
        out_specs=(P(), P(("row", "col"), None)),
        check_vma=False,
    )
```

```python
import functools
import math

import jax
import jax.numpy as jnp
from jax import lax
from jax.experimental import pallas as pl
from jax.experimental.pallas import tpu as pltpu
from jax.sharding import PartitionSpec as P

TILE = 128
PAIR = 2 * TILE
PARTS = 2
MESH = pl.DeviceIdType.MESH
F32 = jnp.float32
BF16 = jnp.bfloat16


def bit_mask(bits, features, across):
    words, nodes = bits.shape
    low = (bits & 255).astype(F32).astype(BF16)
    high = ((bits >> 8) & 255).astype(F32).astype(BF16)
    feature = lax.broadcasted_iota(jnp.int32, (words, features), 1)
    word = lax.broadcasted_iota(jnp.int32, (words, features), 0)
    own = (feature >> 4) == word
    in_low = (feature & 15) < 8
    pick_low = jnp.where(own & in_low, 1.0, 0.0).astype(BF16)
    pick_high = jnp.where(own & ~in_low, 1.0, 0.0).astype(BF16)

    def place(pick, byte):
        left, right = (pick, byte) if across else (byte, pick)
        return lax.dot_general(left, right, (((0,), (0,)), ((), ())), preferred_element_type=F32)

    byte = place(pick_low, low) + place(pick_high, high)
    shift = lax.broadcasted_iota(jnp.int32, byte.shape, 0 if across else 1) & 7
    return (byte.astype(jnp.int32) >> shift) & 1


def flip_bits(index, bits, total):
    result = index
    step = 1
    while step < total:
        if bits & step:
            result = result + step * (1 - 2 * ((index // step) % 2))
        step *= 2
    return result


def exchange(
    rows, cols, scale, grad_hbm, bits_hbm, agg_hbm, weight_hbm, tiles_ref, coords_hbm, count_ref, inbits_hbm,
    out_ref, weight_ref,
    by_col, col_sum, by_row, row_sum, col_total, total_buf,
    w1_send, w1_recv, w2_send, w2_recv, w3_send, w3_recv, w4_send, w4_recv,
    grad_buf, bits_buf, agg_buf, mat_buf, coords_buf, inbits_buf, table_buf, table_ref, hidden_ref, part_ref, load_sem,
    tile_buf, gathered, acc, pair_out, pair_in, chain_out, chain_in, mask_buf,
    tile_sem, hid_send, hid_recv, pair_send, pair_recv, chain_send, chain_recv,
):
    slots = tiles_ref.shape[0]
    nodes, features = grad_hbm.shape
    row_tiles = nodes // TILE
    col_tiles = rows * nodes // TILE
    positions = cols * row_tiles * col_tiles
    pairs_per = nodes // PAIR
    part = features // PARTS
    chips = rows // 2
    my_row = lax.axis_index("row")
    my_col = lax.axis_index("col")
    place = my_row // 2
    core = my_row % 2
    partner = place * 2 + 1 - core

    barrier = pltpu.get_barrier_semaphore()
    peers = [flip_bits(my_col, k, cols) for k in range(cols)]
    mates = [(my_row + i) % rows for i in range(rows)]
    for k in range(1, cols):
        pl.semaphore_signal(barrier, inc=1, device_id=(my_row, peers[k]), device_id_type=MESH)
    for i in range(1, rows):
        pl.semaphore_signal(barrier, inc=1, device_id=(mates[i], my_col), device_id_type=MESH)

    pairs_in = [
        (bits_hbm, bits_buf), (grad_hbm, grad_buf), (weight_hbm, mat_buf),
        (coords_hbm, coords_buf), (inbits_hbm, inbits_buf), (agg_hbm, agg_buf),
    ]
    inputs = [pltpu.make_async_copy(src, dst, load_sem.at[i]) for i, (src, dst) in enumerate(pairs_in)]
    for load in inputs:
        load.start()
    loads = []
    chunk = slots // 8
    for piece in range(8):
        span = pl.ds(piece * chunk, chunk)
        load = pltpu.make_async_copy(tiles_ref.at[span], tile_buf.at[span], tile_sem.at[piece])
        load.start()
        loads.append(load)

    for load in inputs[:3]:
        load.wait()
    mask = bit_mask(bits_buf[...], features, False)
    masked = jnp.where(mask == 1, grad_buf[...].astype(F32), 0.0).astype(BF16)
    hidden_ref[...] = lax.dot_general(
        mat_buf[...], masked, (((1,), (1,)), ((), ())), preferred_element_type=F32
    ).astype(BF16).reshape(PARTS, part, nodes)
    pl.semaphore_wait(barrier, rows + cols - 2)

    def hid_copy(k, p):
        return pltpu.make_async_remote_copy(
            src_ref=hidden_ref.at[p], dst_ref=gathered.at[my_col, p],
            send_sem=hid_send.at[k, p], recv_sem=hid_recv.at[my_col, p],
            device_id=(my_row, peers[k]), device_id_type=MESH,
        )

    def landed(ref, sem):
        pltpu.make_async_copy(ref, ref, sem).wait()

    for k in range(1, cols):
        hid_copy(k, 0).start()

    gathered[my_col] = hidden_ref[...]
    tile_buf[slots] = jnp.zeros((TILE, TILE), BF16)
    for load in inputs[3:]:
        load.wait()
    spot_of = coords_buf[0:1, :] * col_tiles + coords_buf[1:2, :]
    alive = lax.broadcasted_iota(jnp.int32, (1, slots), 1) < count_ref[0, 0]
    spot_of = jnp.where(alive, spot_of, -1)
    spot_of = jnp.broadcast_to(spot_of, (8, slots)).T[:, 0:1]
    wide = min(512, positions)
    for first in range(0, positions, wide):
        spots = lax.broadcasted_iota(jnp.int32, (slots, wide), 1) + first
        slot = lax.broadcasted_iota(jnp.int32, (slots, wide), 0)
        found = jnp.min(jnp.where(spot_of == spots, slot, slots), axis=0, keepdims=True)
        table_buf[:, first:first + wide] = jnp.minimum(jnp.maximum(found, 0), slots)
    to_scalars = pltpu.make_async_copy(table_buf, table_ref, load_sem.at[len(inputs)])
    to_scalars.start()
    part_ref[...] = scale * lax.dot_general(
        agg_buf[...], masked, (((0,), (0,)), ((), ())), preferred_element_type=F32
    )
    mask_buf[...] = bit_mask(inbits_buf[...], features, True).astype(F32)
    to_scalars.wait()
    for load in loads:
        load.wait()

    def product(source, pair, p):
        strips = []
        for i in range(row_tiles):
            base = (source * row_tiles + i) * col_tiles + 2 * pair
            strips.append(
                jnp.concatenate([tile_buf[table_ref[0, base]], tile_buf[table_ref[0, base + 1]]], axis=1)
            )
        return jnp.dot(gathered[source, p], jnp.concatenate(strips, axis=0), preferred_element_type=F32)

    def add_source(k, p):
        if k:
            landed(gathered.at[peers[k], p], hid_recv.at[peers[k], p])

        @pl.loop(0, col_tiles // 2)
        def _(pair):
            value = product(peers[k], pair, p)
            if k:
                value += acc[p, pair]
            acc[p, pair] = value

    band = features // cols
    owners = min(rows, band // 8)
    strip = band // owners

    def w1_copy(k):
        return pltpu.make_async_remote_copy(
            src_ref=part_ref.at[pl.ds(pl.multiple_of(peers[k] * band, 8), band)], dst_ref=by_col.at[my_col],
            send_sem=w1_send.at[k], recv_sem=w1_recv.at[my_col],
            device_id=(my_row, peers[k]), device_id_type=MESH,
        )

    def w2_copy(i):
        return pltpu.make_async_remote_copy(
            src_ref=col_sum.at[pl.ds(pl.multiple_of(mates[i] * strip, 8), strip)], dst_ref=by_row.at[my_row],
            send_sem=w2_send.at[i], recv_sem=w2_recv.at[my_row],
            device_id=(mates[i], my_col), device_id_type=MESH,
        )

    def w3_copy(i):
        return pltpu.make_async_remote_copy(
            src_ref=row_sum, dst_ref=col_total.at[pl.ds(pl.multiple_of(my_row * strip, 8), strip)],
            send_sem=w3_send.at[i], recv_sem=w3_recv.at[my_row],
            device_id=(mates[i], my_col), device_id_type=MESH,
        )

    def w4_copy(k):
        return pltpu.make_async_remote_copy(
            src_ref=col_total, dst_ref=total_buf.at[pl.ds(pl.multiple_of(my_col * band, 8), band)],
            send_sem=w4_send.at[k], recv_sem=w4_recv.at[my_col],
            device_id=(my_row, peers[k]), device_id_type=MESH,
        )

    def weight_one():
        for k in range(1, cols):
            w1_copy(k).start()

    def weight_two():
        total = part_ref[pl.ds(pl.multiple_of(my_col * band, 8), band), :]
        for k in range(1, cols):
            landed(by_col.at[peers[k]], w1_recv.at[peers[k]])
            total += by_col[peers[k]]
        col_sum[...] = total
        for i in range(1, rows):
            @pl.when(mates[i] < owners)
            def _():
                w2_copy(i).start()

    def weight_three():
        @pl.when(my_row < owners)
        def _():
            mine = pl.ds(pl.multiple_of(my_row * strip, 8), strip)
            total = col_sum[mine, :]
            for i in range(1, rows):
                landed(by_row.at[mates[i]], w2_recv.at[mates[i]])
                total += by_row[mates[i]]
            row_sum[...] = total
            col_total[mine, :] = total
            for i in range(1, rows):
                w3_copy(i).start()

    def weight_four():
        for i in range(1, rows):
            @pl.when(mates[i] < owners)
            def _():
                landed(col_total.at[pl.ds(pl.multiple_of(mates[i] * strip, 8), strip)], w3_recv.at[mates[i]])
        total_buf[pl.ds(pl.multiple_of(my_col * band, 8), band), :] = col_total[...]
        for k in range(1, cols):
            w4_copy(k).start()

    def weight_end():
        for k in range(1, cols):
            landed(total_buf.at[pl.ds(pl.multiple_of(peers[k] * band, 8), band)], w4_recv.at[peers[k]])
        weight_ref[...] = total_buf[...]
        for k in range(1, cols):
            w1_copy(k).wait_send()
            w4_copy(k).wait_send()
        for i in range(1, rows):
            @pl.when(mates[i] < owners)
            def _():
                w2_copy(i).wait_send()

            @pl.when(my_row < owners)
            def _():
                w3_copy(i).wait_send()

    order = []
    for d in range((chips + 1) // 2):
        order += [chips - 1 - d] + ([d] if d != chips - 1 - d else [])
    way = place // ((chips + 1) // 2)

    def pair_copy(spot, p):
        return pltpu.make_async_remote_copy(
            src_ref=pair_out.at[p, spot], dst_ref=pair_in.at[p, spot],
            send_sem=pair_send.at[p, spot], recv_sem=pair_recv.at[p, spot],
            device_id=(partner, my_col), device_id_type=MESH,
        )

    def finish(p):
        landed(gathered.at[peers[cols - 1], p], hid_recv.at[peers[cols - 1], p])
        for spot in order:
            for j in range(pairs_per):
                pair = (2 * spot + 1 - core) * pairs_per + j
                value = acc[p, pair] + product(peers[cols - 1], pair, p)
                pair_out[p, spot, :, pl.ds(j * PAIR, PAIR)] = value.astype(BF16)
            pair_copy(spot, p).start()
        for spot in order:
            for j in range(pairs_per):
                pair = (2 * spot + core) * pairs_per + j
                acc[p, pair] += product(peers[cols - 1], pair, p)

    def pair_wait(p):
        for spot in order:
            pair_copy(spot, p).wait_recv()

    def chain_copy(way, spot, p):
        return pltpu.make_async_remote_copy(
            src_ref=chain_out.at[way, spot, p], dst_ref=chain_in.at[way, spot, p],
            send_sem=chain_send.at[way, spot, p], recv_sem=chain_recv.at[way, spot, p],
            device_id=(my_row + 2 - 4 * way, my_col), device_id_type=MESH,
        )

    def local_sum(spot, p):
        first = (2 * spot + core) * pairs_per
        own = jnp.concatenate([acc[p, first + j] for j in range(pairs_per)], axis=1)
        return own + pair_in[p, spot].astype(F32)

    def hop(way, d, p, edge):
        spot = (1 - way) * (chips - 1 - d) + way * d
        ahead = (1 - 2 * way) * (spot - place)
        behind = (1 - way) * place + way * (chips - 1 - place)
        if edge:
            @pl.when((ahead > 0) & (behind == 0))
            def _():
                chain_out[way, spot, p] = local_sum(spot, p).astype(BF16)
                chain_copy(way, spot, p).start()
        else:
            @pl.when((ahead > 0) & (behind > 0))
            def _():
                chain_copy(way, spot, p).wait_recv()
                total = local_sum(spot, p) + chain_in[way, spot, p].astype(F32)
                chain_out[way, spot, p] = total.astype(BF16)
                chain_copy(way, spot, p).start()

    def edge_hops(p):
        pair_wait(p)
        for d in range(chips - 1):
            hop(0, d, p, True)
            hop(1, d, p, True)

    def middle_hops(p, beside):
        for d in range(chips - 1):
            hop(way, d, p, False)
            if d == 0:
                beside()
            hop(1 - way, d, p, False)

    def deliver(p):
        first = (2 * place + core) * pairs_per
        acc_at = [acc.at[p, first + j] for j in range(pairs_per)]
        for j in range(pairs_per):
            acc_at[j][...] += pair_in[p, place, :, pl.ds(j * PAIR, PAIR)].astype(F32)

        @pl.when(place > 0)
        def _():
            chain_copy(0, place, p).wait_recv()
            for j in range(pairs_per):
                acc_at[j][...] += chain_in[0, place, p, :, pl.ds(j * PAIR, PAIR)].astype(F32)

        @pl.when(place < chips - 1)
        def _():
            chain_copy(1, place, p).wait_recv()
            for j in range(pairs_per):
                acc_at[j][...] += chain_in[1, place, p, :, pl.ds(j * PAIR, PAIR)].astype(F32)

        rows_p = pl.ds(p * part, part)
        for j in range(pairs_per):
            span = pl.ds(j * PAIR, PAIR)
            out_ref[span, rows_p] = jnp.where(mask_buf[rows_p, span] > 0.5, acc_at[j][...], 0.0).T.astype(BF16)

    add_source(0, 0)
    for k in range(1, cols):
        hid_copy(k, 0).wait_send()
    for k in range(1, cols):
        hid_copy(k, 1).start()
    weight_one()
    for k in range(1, cols - 1):
        add_source(k, 0)
    finish(0)
    add_source(0, 1)
    edge_hops(0)
    for k in range(1, cols - 1):
        add_source(k, 1)
    finish(1)
    weight_two()
    edge_hops(1)
    middle_hops(0, weight_three)
    middle_hops(1, weight_four)
    for p in range(PARTS):
        deliver(p)
    weight_end()
    for k in range(1, cols):
        hid_copy(k, 1).wait_send()
    for spot in range(chips):
        for p in range(PARTS):
            pair_copy(spot, p).wait_send()

            @pl.when(spot > place)
            def _():
                chain_copy(0, spot, p).wait_send()

            @pl.when(spot < place)
            def _():
                chain_copy(1, spot, p).wait_send()


def shards(out_grad, out_bits, agg_saved, weight, tiles, tile_coords, tile_count, in_bits):
    rows = lax.axis_size("row")
    cols = lax.axis_size("col")
    nodes, features = out_grad.shape
    scale = 1.0 / math.sqrt(nodes * rows * cols)
    slots = tiles.shape[2]
    row_tiles = cols * nodes // TILE
    col_tiles = rows * nodes // TILE
    chips = rows // 2
    part = features // PARTS
    vmem = pl.BlockSpec(memory_space=pltpu.VMEM)
    hbm = pl.BlockSpec(memory_space=pltpu.HBM)

    dma = pltpu.SemaphoreType.DMA
    band = features // cols
    strip = band // min(rows, band // 8)
    prev_grad, weight_grad = pl.pallas_call(
        functools.partial(exchange, rows, cols, scale),
        out_shape=(
            jax.ShapeDtypeStruct((nodes, features), BF16),
            jax.ShapeDtypeStruct((features, features), F32),
        ),
        in_specs=[hbm] * 6 + [pl.BlockSpec(memory_space=pltpu.SMEM), hbm],
        out_specs=(vmem, vmem),
        scratch_shapes=[
            pltpu.VMEM((cols, band, features), F32),
            pltpu.VMEM((band, features), F32),
            pltpu.VMEM((rows, strip, features), F32),
            pltpu.VMEM((strip, features), F32),
            pltpu.VMEM((band, features), F32),
            pltpu.VMEM((features, features), F32),
            dma((cols,)),
            dma((cols,)),
            dma((rows,)),
            dma((rows,)),
            dma((rows,)),
            dma((rows,)),
            dma((cols,)),
            dma((cols,)),
            pltpu.VMEM((nodes, features), BF16),
            pltpu.VMEM((features // 16, nodes), jnp.int32),
            pltpu.VMEM((nodes, features), BF16),
            pltpu.VMEM((features, features), BF16),
            pltpu.VMEM((2, slots), jnp.int32),
            pltpu.VMEM((features // 16, nodes), jnp.int32),
            pltpu.VMEM((1, row_tiles * col_tiles), jnp.int32),
            pltpu.SMEM((1, row_tiles * col_tiles), jnp.int32),
            pltpu.VMEM((PARTS, part, nodes), BF16),
            pltpu.VMEM((features, features), F32),
            dma((7,)),
            pltpu.VMEM((slots + 1, TILE, TILE), BF16),
            pltpu.VMEM((cols, PARTS, part, nodes), BF16),
            pltpu.VMEM((PARTS, col_tiles // 2, part, PAIR), F32),
            pltpu.VMEM((PARTS, chips, part, nodes), BF16),
            pltpu.VMEM((PARTS, chips, part, nodes), BF16),
            pltpu.VMEM((2, chips, PARTS, part, nodes), BF16),
            pltpu.VMEM((2, chips, PARTS, part, nodes), BF16),
            pltpu.VMEM((features, nodes), F32),
            dma((8,)),
            dma((cols, PARTS)),
            dma((cols, PARTS)),
            dma((PARTS, chips)),
            dma((PARTS, chips)),
            dma((2, chips, PARTS)),
            dma((2, chips, PARTS)),
        ],
        compiler_params=pltpu.CompilerParams(
            collective_id=0, has_side_effects=True, vmem_limit_bytes=56 * 2**20
        ),
        cost_estimate=pl.CostEstimate(
            flops=2 * row_tiles * col_tiles * TILE * TILE * features,
            bytes_accessed=slots * TILE * TILE * 2, transcendentals=0,
        ),
        name="exchange",
    )(out_grad, out_bits.T, agg_saved, weight, tiles[0, 0], tile_coords[0, 0].T, tile_count, in_bits.T)
    return weight_grad, prev_grad


def solution(mesh):
    return jax.shard_map(
        shards,
        mesh=mesh,
        in_specs=(
            P(("row", "col"), None),
            P(("row", "col"), None),
            P(("row", "col"), None),
            P(),
            P("row", "col", None, None, None),
            P("row", "col", None, None),
            P("row", "col"),
            P(("row", "col"), None),
        ),
        out_specs=(P(), P(("row", "col"), None)),
        check_vma=False,
    )
```

```python
import functools
import math

import jax
import jax.numpy as jnp
from jax import lax
from jax.experimental import pallas as pl
from jax.experimental.pallas import tpu as pltpu
from jax.sharding import PartitionSpec as P

TILE = 128
PAIR = 2 * TILE
PARTS = 2
MESH = pl.DeviceIdType.MESH
F32 = jnp.float32
BF16 = jnp.bfloat16


def bit_mask(bits, features, across):
    words, nodes = bits.shape
    low = (bits & 255).astype(F32).astype(BF16)
    high = ((bits >> 8) & 255).astype(F32).astype(BF16)
    feature = lax.broadcasted_iota(jnp.int32, (words, features), 1)
    word = lax.broadcasted_iota(jnp.int32, (words, features), 0)
    own = (feature >> 4) == word
    in_low = (feature & 15) < 8
    pick_low = jnp.where(own & in_low, 1.0, 0.0).astype(BF16)
    pick_high = jnp.where(own & ~in_low, 1.0, 0.0).astype(BF16)

    def place(pick, byte):
        left, right = (pick, byte) if across else (byte, pick)
        return lax.dot_general(left, right, (((0,), (0,)), ((), ())), preferred_element_type=F32)

    byte = place(pick_low, low) + place(pick_high, high)
    shift = lax.broadcasted_iota(jnp.int32, byte.shape, 0 if across else 1) & 7
    return (byte.astype(jnp.int32) >> shift) & 1


def flip_bits(index, bits, total):
    result = index
    step = 1
    while step < total:
        if bits & step:
            result = result + step * (1 - 2 * ((index // step) % 2))
        step *= 2
    return result


def exchange(
    rows, cols, scale, grad_hbm, bits_hbm, agg_hbm, weight_hbm, tiles_ref, coords_hbm, count_ref, inbits_hbm,
    out_ref, weight_ref,
    by_col, col_sum, by_row, row_sum, col_total, total_buf,
    w1_send, w1_recv, w2_send, w2_recv, w3_send, w3_recv, w4_send, w4_recv,
    grad_buf, bits_buf, agg_buf, mat_buf, coords_buf, inbits_buf, table_buf, table_ref, hidden_ref, part_ref, load_sem,
    tile_buf, gathered, acc, pair_out, pair_in, chain_out, chain_in, mask_buf,
    tile_sem, hid_send, hid_recv, pair_send, pair_recv, chain_send, chain_recv,
):
    slots = tiles_ref.shape[0]
    nodes, features = grad_hbm.shape
    row_tiles = nodes // TILE
    col_tiles = rows * nodes // TILE
    positions = cols * row_tiles * col_tiles
    pairs_per = nodes // PAIR
    part = features // PARTS
    chips = rows // 2
    my_row = lax.axis_index("row")
    my_col = lax.axis_index("col")
    place = my_row // 2
    core = my_row % 2
    partner = place * 2 + 1 - core

    barrier = pltpu.get_barrier_semaphore()
    peers = [flip_bits(my_col, k, cols) for k in range(cols)]
    mates = [(my_row + i) % rows for i in range(rows)]
    for k in range(1, cols):
        pl.semaphore_signal(barrier, inc=1, device_id=(my_row, peers[k]), device_id_type=MESH)
    for i in range(1, rows):
        pl.semaphore_signal(barrier, inc=1, device_id=(mates[i], my_col), device_id_type=MESH)

    pairs_in = [
        (bits_hbm, bits_buf), (grad_hbm, grad_buf), (weight_hbm, mat_buf),
        (coords_hbm, coords_buf), (inbits_hbm, inbits_buf), (agg_hbm, agg_buf),
    ]
    inputs = [pltpu.make_async_copy(src, dst, load_sem.at[i]) for i, (src, dst) in enumerate(pairs_in)]
    for load in inputs:
        load.start()
    loads = []
    chunk = slots // 8
    for piece in range(8):
        span = pl.ds(piece * chunk, chunk)
        load = pltpu.make_async_copy(tiles_ref.at[span], tile_buf.at[span], tile_sem.at[piece])
        load.start()
        loads.append(load)

    for load in inputs[:3]:
        load.wait()
    mask = bit_mask(bits_buf[...], features, False)
    masked = jnp.where(mask == 1, grad_buf[...].astype(F32), 0.0).astype(BF16)
    hidden_ref[...] = lax.dot_general(
        mat_buf[...], masked, (((1,), (1,)), ((), ())), preferred_element_type=F32
    ).astype(BF16).reshape(PARTS, part, nodes)
    pl.semaphore_wait(barrier, rows + cols - 2)

    def hid_copy(k, p):
        return pltpu.make_async_remote_copy(
            src_ref=hidden_ref.at[p], dst_ref=gathered.at[my_col, p],
            send_sem=hid_send.at[k, p], recv_sem=hid_recv.at[my_col, p],
            device_id=(my_row, peers[k]), device_id_type=MESH,
        )

    def landed(ref, sem):
        pltpu.make_async_copy(ref, ref, sem).wait()

    near = range(1, cols - 1)
    far = range(cols - 1, cols)

    def send(group, p):
        for k in group:
            hid_copy(k, p).start()

    def sent(group, p):
        for k in group:
            hid_copy(k, p).wait_send()

    send(near, 0)
    gathered[my_col] = hidden_ref[...]
    tile_buf[slots] = jnp.zeros((TILE, TILE), BF16)
    for load in inputs[3:]:
        load.wait()
    spot_of = coords_buf[0:1, :] * col_tiles + coords_buf[1:2, :]
    alive = lax.broadcasted_iota(jnp.int32, (1, slots), 1) < count_ref[0, 0]
    spot_of = jnp.where(alive, spot_of, -1)
    spot_of = jnp.broadcast_to(spot_of, (8, slots)).T[:, 0:1]
    wide = min(512, positions)
    for first in range(0, positions, wide):
        spots = lax.broadcasted_iota(jnp.int32, (slots, wide), 1) + first
        slot = lax.broadcasted_iota(jnp.int32, (slots, wide), 0)
        found = jnp.min(jnp.where(spot_of == spots, slot, slots), axis=0, keepdims=True)
        table_buf[:, first:first + wide] = jnp.minimum(jnp.maximum(found, 0), slots)
    to_scalars = pltpu.make_async_copy(table_buf, table_ref, load_sem.at[len(inputs)])
    to_scalars.start()
    part_ref[...] = scale * lax.dot_general(
        agg_buf[...], masked, (((0,), (0,)), ((), ())), preferred_element_type=F32
    )
    mask_buf[...] = bit_mask(inbits_buf[...], features, True).astype(F32)
    sent(near, 0)
    send(far, 0)
    to_scalars.wait()
    for load in loads:
        load.wait()

    def product(source, pair, p):
        strips = []
        for i in range(row_tiles):
            base = (source * row_tiles + i) * col_tiles + 2 * pair
            strips.append(
                jnp.concatenate([tile_buf[table_ref[0, base]], tile_buf[table_ref[0, base + 1]]], axis=1)
            )
        return jnp.dot(gathered[source, p], jnp.concatenate(strips, axis=0), preferred_element_type=F32)

    def add_sources(group, p):
        for k in group:
            if k:
                landed(gathered.at[peers[k], p], hid_recv.at[peers[k], p])

        @pl.loop(0, col_tiles // 2, unroll=4)
        def _(pair):
            value = product(peers[group[0]], pair, p)
            for k in group[1:]:
                value += product(peers[k], pair, p)
            if group[0]:
                value += acc[p, pair]
            acc[p, pair] = value

    band = features // cols
    owners = min(rows, band // 8)
    strip = band // owners

    def w1_copy(k):
        return pltpu.make_async_remote_copy(
            src_ref=part_ref.at[pl.ds(pl.multiple_of(peers[k] * band, 8), band)], dst_ref=by_col.at[my_col],
            send_sem=w1_send.at[k], recv_sem=w1_recv.at[my_col],
            device_id=(my_row, peers[k]), device_id_type=MESH,
        )

    def w2_copy(i):
        return pltpu.make_async_remote_copy(
            src_ref=col_sum.at[pl.ds(pl.multiple_of(mates[i] * strip, 8), strip)], dst_ref=by_row.at[my_row],
            send_sem=w2_send.at[i], recv_sem=w2_recv.at[my_row],
            device_id=(mates[i], my_col), device_id_type=MESH,
        )

    def w3_copy(i):
        return pltpu.make_async_remote_copy(
            src_ref=row_sum, dst_ref=col_total.at[pl.ds(pl.multiple_of(my_row * strip, 8), strip)],
            send_sem=w3_send.at[i], recv_sem=w3_recv.at[my_row],
            device_id=(mates[i], my_col), device_id_type=MESH,
        )

    def w4_copy(k):
        return pltpu.make_async_remote_copy(
            src_ref=col_total, dst_ref=total_buf.at[pl.ds(pl.multiple_of(my_col * band, 8), band)],
            send_sem=w4_send.at[k], recv_sem=w4_recv.at[my_col],
            device_id=(my_row, peers[k]), device_id_type=MESH,
        )

    def weight_one():
        for k in range(1, cols):
            w1_copy(k).start()

    def weight_two():
        total = part_ref[pl.ds(pl.multiple_of(my_col * band, 8), band), :]
        for k in range(1, cols):
            landed(by_col.at[peers[k]], w1_recv.at[peers[k]])
            total += by_col[peers[k]]
        col_sum[...] = total
        for i in range(1, rows):
            @pl.when(mates[i] < owners)
            def _():
                w2_copy(i).start()

    def weight_three():
        @pl.when(my_row < owners)
        def _():
            mine = pl.ds(pl.multiple_of(my_row * strip, 8), strip)
            total = col_sum[mine, :]
            for i in range(1, rows):
                landed(by_row.at[mates[i]], w2_recv.at[mates[i]])
                total += by_row[mates[i]]
            row_sum[...] = total
            col_total[mine, :] = total
            for i in range(1, rows):
                w3_copy(i).start()

    def weight_four():
        for i in range(1, rows):
            @pl.when(mates[i] < owners)
            def _():
                landed(col_total.at[pl.ds(pl.multiple_of(mates[i] * strip, 8), strip)], w3_recv.at[mates[i]])
        total_buf[pl.ds(pl.multiple_of(my_col * band, 8), band), :] = col_total[...]
        for k in range(1, cols):
            w4_copy(k).start()

    def weight_end():
        for k in range(1, cols):
            landed(total_buf.at[pl.ds(pl.multiple_of(peers[k] * band, 8), band)], w4_recv.at[peers[k]])
        weight_ref[...] = total_buf[...]
        for k in range(1, cols):
            w1_copy(k).wait_send()
            w4_copy(k).wait_send()
        for i in range(1, rows):
            @pl.when(mates[i] < owners)
            def _():
                w2_copy(i).wait_send()

            @pl.when(my_row < owners)
            def _():
                w3_copy(i).wait_send()

    order = []
    for d in range((chips + 1) // 2):
        order += [chips - 1 - d] + ([d] if d != chips - 1 - d else [])
    way = place // ((chips + 1) // 2)

    def pair_copy(spot, p):
        return pltpu.make_async_remote_copy(
            src_ref=pair_out.at[p, spot], dst_ref=pair_in.at[p, spot],
            send_sem=pair_send.at[p, spot], recv_sem=pair_recv.at[p, spot],
            device_id=(partner, my_col), device_id_type=MESH,
        )

    def finish(p):
        landed(gathered.at[peers[cols - 1], p], hid_recv.at[peers[cols - 1], p])
        for spot in order:
            for j in range(pairs_per):
                pair = (2 * spot + 1 - core) * pairs_per + j
                value = acc[p, pair] + product(peers[cols - 1], pair, p)
                pair_out[p, spot, :, pl.ds(j * PAIR, PAIR)] = value.astype(BF16)
            pair_copy(spot, p).start()
        for spot in order:
            for j in range(pairs_per):
                pair = (2 * spot + core) * pairs_per + j
                acc[p, pair] += product(peers[cols - 1], pair, p)

    def pair_wait(p):
        for spot in order:
            pair_copy(spot, p).wait_recv()

    def chain_copy(way, spot, p):
        return pltpu.make_async_remote_copy(
            src_ref=chain_out.at[way, spot, p], dst_ref=chain_in.at[way, spot, p],
            send_sem=chain_send.at[way, spot, p], recv_sem=chain_recv.at[way, spot, p],
            device_id=(my_row + 2 - 4 * way, my_col), device_id_type=MESH,
        )

    def local_sum(spot, p):
        first = (2 * spot + core) * pairs_per
        own = jnp.concatenate([acc[p, first + j] for j in range(pairs_per)], axis=1)
        return own + pair_in[p, spot].astype(F32)

    def hop(way, d, p, edge):
        spot = (1 - way) * (chips - 1 - d) + way * d
        ahead = (1 - 2 * way) * (spot - place)
        behind = (1 - way) * place + way * (chips - 1 - place)
        if edge:
            @pl.when((ahead > 0) & (behind == 0))
            def _():
                chain_out[way, spot, p] = local_sum(spot, p).astype(BF16)
                chain_copy(way, spot, p).start()
        else:
            @pl.when((ahead > 0) & (behind > 0))
            def _():
                chain_copy(way, spot, p).wait_recv()
                total = local_sum(spot, p) + chain_in[way, spot, p].astype(F32)
                chain_out[way, spot, p] = total.astype(BF16)
                chain_copy(way, spot, p).start()

    def edge_hops(p):
        pair_wait(p)
        for d in range(chips - 1):
            hop(0, d, p, True)
            hop(1, d, p, True)

    def middle_hops(p, beside):
        for d in range(chips - 1):
            hop(way, d, p, False)
            if d == 0:
                beside()
            hop(1 - way, d, p, False)

    def deliver(p):
        first = (2 * place + core) * pairs_per
        acc_at = [acc.at[p, first + j] for j in range(pairs_per)]
        for j in range(pairs_per):
            acc_at[j][...] += pair_in[p, place, :, pl.ds(j * PAIR, PAIR)].astype(F32)

        @pl.when(place > 0)
        def _():
            chain_copy(0, place, p).wait_recv()
            for j in range(pairs_per):
                acc_at[j][...] += chain_in[0, place, p, :, pl.ds(j * PAIR, PAIR)].astype(F32)

        @pl.when(place < chips - 1)
        def _():
            chain_copy(1, place, p).wait_recv()
            for j in range(pairs_per):
                acc_at[j][...] += chain_in[1, place, p, :, pl.ds(j * PAIR, PAIR)].astype(F32)

        rows_p = pl.ds(p * part, part)
        for j in range(pairs_per):
            span = pl.ds(j * PAIR, PAIR)
            out_ref[span, rows_p] = jnp.where(mask_buf[rows_p, span] > 0.5, acc_at[j][...], 0.0).T.astype(BF16)

    add_sources([0], 0)
    sent(far, 0)
    send(near, 1)
    add_sources(near, 0)
    finish(0)
    sent(near, 1)
    send(far, 1)
    weight_one()
    add_sources([0], 1)
    edge_hops(0)
    add_sources(near, 1)
    finish(1)
    weight_two()
    edge_hops(1)
    middle_hops(0, weight_three)
    middle_hops(1, weight_four)
    for p in range(PARTS):
        deliver(p)
    weight_end()
    sent(far, 1)
    for spot in range(chips):
        for p in range(PARTS):
            pair_copy(spot, p).wait_send()

            @pl.when(spot > place)
            def _():
                chain_copy(0, spot, p).wait_send()

            @pl.when(spot < place)
            def _():
                chain_copy(1, spot, p).wait_send()


def deliver_all(prev_in, weight_in, prev_out, weight_out, sems):
    copies = []
    for i, (src, dst) in enumerate(((prev_in, prev_out), (weight_in, weight_out))):
        chunk = src.shape[0] // 4
        for j in range(4):
            span = pl.ds(j * chunk, chunk)
            copies.append(pltpu.make_async_copy(src.at[span], dst.at[span], sems.at[i, j]))
            copies[-1].start()
    for copy in copies:
        copy.wait()


def shards(out_grad, out_bits, agg_saved, weight, tiles, tile_coords, tile_count, in_bits):
    rows = lax.axis_size("row")
    cols = lax.axis_size("col")
    nodes, features = out_grad.shape
    scale = 1.0 / math.sqrt(nodes * rows * cols)
    slots = tiles.shape[2]
    row_tiles = cols * nodes // TILE
    col_tiles = rows * nodes // TILE
    chips = rows // 2
    part = features // PARTS
    vmem = pl.BlockSpec(memory_space=pltpu.VMEM)
    hbm = pl.BlockSpec(memory_space=pltpu.HBM)

    dma = pltpu.SemaphoreType.DMA
    band = features // cols
    strip = band // min(rows, band // 8)
    prev_grad, weight_grad = pl.pallas_call(
        functools.partial(exchange, rows, cols, scale),
        out_shape=(
            jax.ShapeDtypeStruct((nodes, features), BF16),
            jax.ShapeDtypeStruct((features, features), F32),
        ),
        in_specs=[hbm] * 6 + [pl.BlockSpec(memory_space=pltpu.SMEM), hbm],
        out_specs=(vmem, vmem),
        scratch_shapes=[
            pltpu.VMEM((cols, band, features), F32),
            pltpu.VMEM((band, features), F32),
            pltpu.VMEM((rows, strip, features), F32),
            pltpu.VMEM((strip, features), F32),
            pltpu.VMEM((band, features), F32),
            pltpu.VMEM((features, features), F32),
            dma((cols,)),
            dma((cols,)),
            dma((rows,)),
            dma((rows,)),
            dma((rows,)),
            dma((rows,)),
            dma((cols,)),
            dma((cols,)),
            pltpu.VMEM((nodes, features), BF16),
            pltpu.VMEM((features // 16, nodes), jnp.int32),
            pltpu.VMEM((nodes, features), BF16),
            pltpu.VMEM((features, features), BF16),
            pltpu.VMEM((2, slots), jnp.int32),
            pltpu.VMEM((features // 16, nodes), jnp.int32),
            pltpu.VMEM((1, row_tiles * col_tiles), jnp.int32),
            pltpu.SMEM((1, row_tiles * col_tiles), jnp.int32),
            pltpu.VMEM((PARTS, part, nodes), BF16),
            pltpu.VMEM((features, features), F32),
            dma((7,)),
            pltpu.VMEM((slots + 1, TILE, TILE), BF16),
            pltpu.VMEM((cols, PARTS, part, nodes), BF16),
            pltpu.VMEM((PARTS, col_tiles // 2, part, PAIR), F32),
            pltpu.VMEM((PARTS, chips, part, nodes), BF16),
            pltpu.VMEM((PARTS, chips, part, nodes), BF16),
            pltpu.VMEM((2, chips, PARTS, part, nodes), BF16),
            pltpu.VMEM((2, chips, PARTS, part, nodes), BF16),
            pltpu.VMEM((features, nodes), F32),
            dma((8,)),
            dma((cols, PARTS)),
            dma((cols, PARTS)),
            dma((PARTS, chips)),
            dma((PARTS, chips)),
            dma((2, chips, PARTS)),
            dma((2, chips, PARTS)),
        ],
        compiler_params=pltpu.CompilerParams(
            collective_id=0, has_side_effects=True, vmem_limit_bytes=56 * 2**20
        ),
        cost_estimate=pl.CostEstimate(
            flops=2 * row_tiles * col_tiles * TILE * TILE * features,
            bytes_accessed=slots * TILE * TILE * 2, transcendentals=0,
        ),
        name="exchange",
    )(out_grad, out_bits.T, agg_saved, weight, tiles[0, 0], tile_coords[0, 0].T, tile_count, in_bits.T)
    hbm_out = pl.BlockSpec(memory_space=pl.ANY)
    prev_grad, weight_grad = pl.pallas_call(
        deliver_all,
        out_shape=(
            jax.ShapeDtypeStruct((nodes, features), BF16),
            jax.ShapeDtypeStruct((features, features), F32),
        ),
        in_specs=[hbm_out] * 2,
        out_specs=(hbm_out, hbm_out),
        scratch_shapes=[dma((2, 4))],
        compiler_params=pltpu.CompilerParams(vmem_limit_bytes=56 * 2**20),
        name="deliver",
    )(prev_grad, weight_grad)
    return weight_grad, prev_grad


def solution(mesh):
    return jax.shard_map(
        shards,
        mesh=mesh,
        in_specs=(
            P(("row", "col"), None),
            P(("row", "col"), None),
            P(("row", "col"), None),
            P(),
            P("row", "col", None, None, None),
            P("row", "col", None, None),
            P("row", "col"),
            P(("row", "col"), None),
        ),
        out_specs=(P(), P(("row", "col"), None)),
        check_vma=False,
    )
```

```python
import functools
import math

import jax
import jax.numpy as jnp
from jax import lax
from jax.experimental import pallas as pl
from jax.experimental.pallas import tpu as pltpu
from jax.sharding import PartitionSpec as P

TILE = 128
PAIR = 2 * TILE
PARTS = 2
MESH = pl.DeviceIdType.MESH
F32 = jnp.float32
BF16 = jnp.bfloat16


def bit_mask(bits, features, across):
    words, nodes = bits.shape
    low = (bits & 255).astype(F32).astype(BF16)
    high = ((bits >> 8) & 255).astype(F32).astype(BF16)
    feature = lax.broadcasted_iota(jnp.int32, (words, features), 1)
    word = lax.broadcasted_iota(jnp.int32, (words, features), 0)
    own = (feature >> 4) == word
    in_low = (feature & 15) < 8
    pick_low = jnp.where(own & in_low, 1.0, 0.0).astype(BF16)
    pick_high = jnp.where(own & ~in_low, 1.0, 0.0).astype(BF16)

    def place(pick, byte):
        left, right = (pick, byte) if across else (byte, pick)
        return lax.dot_general(left, right, (((0,), (0,)), ((), ())), preferred_element_type=F32)

    byte = place(pick_low, low) + place(pick_high, high)
    shift = lax.broadcasted_iota(jnp.int32, byte.shape, 0 if across else 1) & 7
    return (byte.astype(jnp.int32) >> shift) & 1


def flip_bits(index, bits, total):
    result = index
    step = 1
    while step < total:
        if bits & step:
            result = result + step * (1 - 2 * ((index // step) % 2))
        step *= 2
    return result


def exchange(
    rows, cols, scale, grad_hbm, bits_hbm, agg_hbm, weight_hbm, tiles_ref, coords_hbm, count_ref, inbits_hbm,
    out_ref, weight_ref,
    by_col, col_sum, by_row, row_sum, col_total, total_buf,
    w1_send, w1_recv, w2_send, w2_recv, w3_send, w3_recv, w4_send, w4_recv,
    grad_buf, bits_buf, agg_buf, mat_buf, coords_buf, inbits_buf, table_buf, table_ref, hidden_ref, part_ref, load_sem,
    tile_buf, gathered, acc, pair_out, pair_in, chain_out, chain_in, mask_buf,
    tile_sem, hid_send, hid_recv, pair_send, pair_recv, chain_send, chain_recv,
):
    slots = tiles_ref.shape[0]
    nodes, features = grad_hbm.shape
    row_tiles = nodes // TILE
    col_tiles = rows * nodes // TILE
    positions = cols * row_tiles * col_tiles
    pairs_per = nodes // PAIR
    part = features // PARTS
    chips = rows // 2
    my_row = lax.axis_index("row")
    my_col = lax.axis_index("col")
    place = my_row // 2
    core = my_row % 2
    partner = place * 2 + 1 - core

    barrier = pltpu.get_barrier_semaphore()
    peers = [flip_bits(my_col, k, cols) for k in range(cols)]
    mates = [(my_row + i) % rows for i in range(rows)]
    for k in range(1, cols):
        pl.semaphore_signal(barrier, inc=1, device_id=(my_row, peers[k]), device_id_type=MESH)
    for i in range(1, rows):
        pl.semaphore_signal(barrier, inc=1, device_id=(mates[i], my_col), device_id_type=MESH)

    pairs_in = [
        (bits_hbm, bits_buf), (grad_hbm, grad_buf), (weight_hbm, mat_buf),
        (coords_hbm, coords_buf), (inbits_hbm, inbits_buf), (agg_hbm, agg_buf),
    ]
    inputs = [pltpu.make_async_copy(src, dst, load_sem.at[i]) for i, (src, dst) in enumerate(pairs_in)]
    for load in inputs:
        load.start()
    loads = []
    chunk = slots // 8
    for piece in range(8):
        span = pl.ds(piece * chunk, chunk)
        load = pltpu.make_async_copy(tiles_ref.at[span], tile_buf.at[span], tile_sem.at[piece])
        load.start()
        loads.append(load)

    for load in inputs[:3]:
        load.wait()
    mask = bit_mask(bits_buf[...], features, False)
    masked = jnp.where(mask == 1, grad_buf[...].astype(F32), 0.0).astype(BF16)
    hidden_ref[...] = lax.dot_general(
        mat_buf[...], masked, (((1,), (1,)), ((), ())), preferred_element_type=F32
    ).astype(BF16).reshape(PARTS, part, nodes)
    pl.semaphore_wait(barrier, rows + cols - 2)

    def hid_copy(k, p):
        return pltpu.make_async_remote_copy(
            src_ref=hidden_ref.at[p], dst_ref=gathered.at[my_col, p],
            send_sem=hid_send.at[k, p], recv_sem=hid_recv.at[my_col, p],
            device_id=(my_row, peers[k]), device_id_type=MESH,
        )

    def landed(ref, sem):
        pltpu.make_async_copy(ref, ref, sem).wait()

    near = range(1, cols - 1)
    far = range(cols - 1, cols)

    def send(group, p):
        for k in group:
            hid_copy(k, p).start()

    def sent(group, p):
        for k in group:
            hid_copy(k, p).wait_send()

    send(near, 0)
    tile_buf[slots] = jnp.zeros((TILE, TILE), BF16)
    for load in inputs[3:]:
        load.wait()
    spot_of = coords_buf[0:1, :] * col_tiles + coords_buf[1:2, :]
    alive = lax.broadcasted_iota(jnp.int32, (1, slots), 1) < count_ref[0, 0]
    spot_of = jnp.where(alive, spot_of, -1)
    spot_of = jnp.broadcast_to(spot_of, (8, slots)).T[:, 0:1]
    wide = min(512, positions)
    for first in range(0, positions, wide):
        spots = lax.broadcasted_iota(jnp.int32, (slots, wide), 1) + first
        slot = lax.broadcasted_iota(jnp.int32, (slots, wide), 0)
        found = jnp.min(jnp.where(spot_of == spots, slot, slots), axis=0, keepdims=True)
        table_buf[:, first:first + wide] = jnp.minimum(jnp.maximum(found, 0), slots)
    to_scalars = pltpu.make_async_copy(table_buf, table_ref, load_sem.at[len(inputs)])
    to_scalars.start()
    part_ref[...] = scale * lax.dot_general(
        agg_buf[...], masked, (((0,), (0,)), ((), ())), preferred_element_type=F32
    )
    mask_buf[...] = bit_mask(inbits_buf[...], features, True).astype(F32)
    sent(near, 0)
    send(far, 0)
    to_scalars.wait()
    for load in loads:
        load.wait()

    def product(source, pair, p=None):
        strips = []
        for i in range(row_tiles):
            base = (source * row_tiles + i) * col_tiles + 2 * pair
            strips.append(
                jnp.concatenate([tile_buf[table_ref[0, base]], tile_buf[table_ref[0, base + 1]]], axis=1)
            )
        left = hidden_ref[...].reshape(features, nodes) if p is None else gathered[source, p]
        return jnp.dot(left, jnp.concatenate(strips, axis=0), preferred_element_type=F32)

    def own_source():
        @pl.loop(0, col_tiles // 2, unroll=4)
        def _(pair):
            value = product(my_col, pair)
            for p in range(PARTS):
                acc[p, pair] = value[p * part:(p + 1) * part]

    def add_sources(group, p):
        for k in group:
            landed(gathered.at[peers[k], p], hid_recv.at[peers[k], p])

        @pl.loop(0, col_tiles // 2, unroll=4)
        def _(pair):
            value = product(peers[group[0]], pair, p)
            for k in group[1:]:
                value += product(peers[k], pair, p)
            acc[p, pair] += value

    band = features // cols
    owners = min(rows, band // 8)
    strip = band // owners

    def w1_copy(k):
        return pltpu.make_async_remote_copy(
            src_ref=part_ref.at[pl.ds(pl.multiple_of(peers[k] * band, 8), band)], dst_ref=by_col.at[my_col],
            send_sem=w1_send.at[k], recv_sem=w1_recv.at[my_col],
            device_id=(my_row, peers[k]), device_id_type=MESH,
        )

    def w2_copy(i):
        return pltpu.make_async_remote_copy(
            src_ref=col_sum.at[pl.ds(pl.multiple_of(mates[i] * strip, 8), strip)], dst_ref=by_row.at[my_row],
            send_sem=w2_send.at[i], recv_sem=w2_recv.at[my_row],
            device_id=(mates[i], my_col), device_id_type=MESH,
        )

    def w3_copy(i):
        return pltpu.make_async_remote_copy(
            src_ref=row_sum, dst_ref=col_total.at[pl.ds(pl.multiple_of(my_row * strip, 8), strip)],
            send_sem=w3_send.at[i], recv_sem=w3_recv.at[my_row],
            device_id=(mates[i], my_col), device_id_type=MESH,
        )

    def w4_copy(k):
        return pltpu.make_async_remote_copy(
            src_ref=col_total, dst_ref=total_buf.at[pl.ds(pl.multiple_of(my_col * band, 8), band)],
            send_sem=w4_send.at[k], recv_sem=w4_recv.at[my_col],
            device_id=(my_row, peers[k]), device_id_type=MESH,
        )

    def weight_one():
        for k in range(1, cols):
            w1_copy(k).start()

    def weight_two():
        total = part_ref[pl.ds(pl.multiple_of(my_col * band, 8), band), :]
        for k in range(1, cols):
            landed(by_col.at[peers[k]], w1_recv.at[peers[k]])
            total += by_col[peers[k]]
        col_sum[...] = total
        for i in range(1, rows):
            @pl.when(mates[i] < owners)
            def _():
                w2_copy(i).start()

    def weight_three():
        @pl.when(my_row < owners)
        def _():
            mine = pl.ds(pl.multiple_of(my_row * strip, 8), strip)
            total = col_sum[mine, :]
            for i in range(1, rows):
                landed(by_row.at[mates[i]], w2_recv.at[mates[i]])
                total += by_row[mates[i]]
            row_sum[...] = total
            col_total[mine, :] = total
            for i in range(1, rows):
                w3_copy(i).start()

    def weight_four():
        for i in range(1, rows):
            @pl.when(mates[i] < owners)
            def _():
                landed(col_total.at[pl.ds(pl.multiple_of(mates[i] * strip, 8), strip)], w3_recv.at[mates[i]])
        total_buf[pl.ds(pl.multiple_of(my_col * band, 8), band), :] = col_total[...]
        for k in range(1, cols):
            w4_copy(k).start()

    def weight_end():
        for k in range(1, cols):
            landed(total_buf.at[pl.ds(pl.multiple_of(peers[k] * band, 8), band)], w4_recv.at[peers[k]])
        weight_ref[...] = total_buf[...]
        for k in range(1, cols):
            w1_copy(k).wait_send()
            w4_copy(k).wait_send()
        for i in range(1, rows):
            @pl.when(mates[i] < owners)
            def _():
                w2_copy(i).wait_send()

            @pl.when(my_row < owners)
            def _():
                w3_copy(i).wait_send()

    order = []
    for d in range((chips + 1) // 2):
        order += [chips - 1 - d] + ([d] if d != chips - 1 - d else [])
    way = place // ((chips + 1) // 2)

    def pair_copy(spot, p):
        return pltpu.make_async_remote_copy(
            src_ref=pair_out.at[p, spot], dst_ref=pair_in.at[p, spot],
            send_sem=pair_send.at[p, spot], recv_sem=pair_recv.at[p, spot],
            device_id=(partner, my_col), device_id_type=MESH,
        )

    def finish(p):
        landed(gathered.at[peers[cols - 1], p], hid_recv.at[peers[cols - 1], p])
        for spot in order:
            for j in range(pairs_per):
                pair = (2 * spot + 1 - core) * pairs_per + j
                value = acc[p, pair] + product(peers[cols - 1], pair, p)
                pair_out[p, spot, :, pl.ds(j * PAIR, PAIR)] = value.astype(BF16)
            pair_copy(spot, p).start()
        for spot in order:
            for j in range(pairs_per):
                pair = (2 * spot + core) * pairs_per + j
                acc[p, pair] += product(peers[cols - 1], pair, p)

    def chain_copy(way, spot, p):
        return pltpu.make_async_remote_copy(
            src_ref=chain_out.at[way, spot, p], dst_ref=chain_in.at[way, spot, p],
            send_sem=chain_send.at[way, spot, p], recv_sem=chain_recv.at[way, spot, p],
            device_id=(my_row + 2 - 4 * way, my_col), device_id_type=MESH,
        )

    def local_sum(spot, p):
        first = (2 * spot + core) * pairs_per
        own = jnp.concatenate([acc[p, first + j] for j in range(pairs_per)], axis=1)
        return own + pair_in[p, spot].astype(F32)

    def hop(way, d, p, edge):
        spot = (1 - way) * (chips - 1 - d) + way * d
        ahead = (1 - 2 * way) * (spot - place)
        behind = (1 - way) * place + way * (chips - 1 - place)
        if edge:
            @pl.when((ahead > 0) & (behind == 0))
            def _():
                pair_copy(spot, p).wait_recv()
                chain_out[way, spot, p] = local_sum(spot, p).astype(BF16)
                chain_copy(way, spot, p).start()
        else:
            @pl.when((ahead > 0) & (behind > 0))
            def _():
                pair_copy(spot, p).wait_recv()
                chain_copy(way, spot, p).wait_recv()
                total = local_sum(spot, p) + chain_in[way, spot, p].astype(F32)
                chain_out[way, spot, p] = total.astype(BF16)
                chain_copy(way, spot, p).start()

    def edge_hops(p):
        for d in range(chips - 1):
            hop(0, d, p, True)
            hop(1, d, p, True)

    def middle_hops(p, beside):
        for d in range(chips - 1):
            if d or p:
                hop(way, d, p, False)
            if d == 0:
                beside()
            hop(1 - way, d, p, False)

    def deliver(p):
        first = (2 * place + core) * pairs_per
        acc_at = [acc.at[p, first + j] for j in range(pairs_per)]
        pair_copy(place, p).wait_recv()
        for j in range(pairs_per):
            acc_at[j][...] += pair_in[p, place, :, pl.ds(j * PAIR, PAIR)].astype(F32)

        @pl.when(place > 0)
        def _():
            chain_copy(0, place, p).wait_recv()
            for j in range(pairs_per):
                acc_at[j][...] += chain_in[0, place, p, :, pl.ds(j * PAIR, PAIR)].astype(F32)

        @pl.when(place < chips - 1)
        def _():
            chain_copy(1, place, p).wait_recv()
            for j in range(pairs_per):
                acc_at[j][...] += chain_in[1, place, p, :, pl.ds(j * PAIR, PAIR)].astype(F32)

        rows_p = pl.ds(p * part, part)
        for j in range(pairs_per):
            span = pl.ds(j * PAIR, PAIR)
            out_ref[span, rows_p] = jnp.where(mask_buf[rows_p, span] > 0.5, acc_at[j][...], 0.0).T.astype(BF16)

    own_source()
    sent(far, 0)
    send(near, 1)
    add_sources(near, 0)
    finish(0)
    sent(near, 1)
    send(far, 1)
    edge_hops(0)
    weight_one()
    add_sources(near, 1)
    hop(way, 0, 0, False)
    finish(1)
    weight_two()
    edge_hops(1)
    middle_hops(0, weight_three)
    middle_hops(1, weight_four)
    for p in range(PARTS):
        deliver(p)
    weight_end()
    sent(far, 1)
    for spot in range(chips):
        for p in range(PARTS):
            pair_copy(spot, p).wait_send()

            @pl.when(spot > place)
            def _():
                chain_copy(0, spot, p).wait_send()

            @pl.when(spot < place)
            def _():
                chain_copy(1, spot, p).wait_send()


def deliver_all(prev_in, weight_in, prev_out, weight_out, prev_buf, weight_buf, sems):
    inward, outward = [], []
    for i, (src, buf, dst) in enumerate(((prev_in, prev_buf, prev_out), (weight_in, weight_buf, weight_out))):
        chunk = src.shape[0] // 4
        for j in range(4):
            span = pl.ds(j * chunk, chunk)
            inward.append(pltpu.make_async_copy(src.at[span], buf.at[span], sems.at[0, i, j]))
            outward.append(pltpu.make_async_copy(buf.at[span], dst.at[span], sems.at[1, i, j]))
    for copy in inward:
        copy.start()
    for first, second in zip(inward, outward):
        first.wait()
        second.start()
    for copy in outward:
        copy.wait()


def shards(out_grad, out_bits, agg_saved, weight, tiles, tile_coords, tile_count, in_bits):
    rows = lax.axis_size("row")
    cols = lax.axis_size("col")
    nodes, features = out_grad.shape
    scale = 1.0 / math.sqrt(nodes * rows * cols)
    slots = tiles.shape[2]
    row_tiles = cols * nodes // TILE
    col_tiles = rows * nodes // TILE
    chips = rows // 2
    part = features // PARTS
    vmem = pl.BlockSpec(memory_space=pltpu.VMEM)
    hbm = pl.BlockSpec(memory_space=pltpu.HBM)

    dma = pltpu.SemaphoreType.DMA
    band = features // cols
    strip = band // min(rows, band // 8)
    prev_grad, weight_grad = pl.pallas_call(
        functools.partial(exchange, rows, cols, scale),
        out_shape=(
            jax.ShapeDtypeStruct((nodes, features), BF16),
            jax.ShapeDtypeStruct((features, features), F32),
        ),
        in_specs=[hbm] * 6 + [pl.BlockSpec(memory_space=pltpu.SMEM), hbm],
        out_specs=(vmem, vmem),
        scratch_shapes=[
            pltpu.VMEM((cols, band, features), F32),
            pltpu.VMEM((band, features), F32),
            pltpu.VMEM((rows, strip, features), F32),
            pltpu.VMEM((strip, features), F32),
            pltpu.VMEM((band, features), F32),
            pltpu.VMEM((features, features), F32),
            dma((cols,)),
            dma((cols,)),
            dma((rows,)),
            dma((rows,)),
            dma((rows,)),
            dma((rows,)),
            dma((cols,)),
            dma((cols,)),
            pltpu.VMEM((nodes, features), BF16),
            pltpu.VMEM((features // 16, nodes), jnp.int32),
            pltpu.VMEM((nodes, features), BF16),
            pltpu.VMEM((features, features), BF16),
            pltpu.VMEM((2, slots), jnp.int32),
            pltpu.VMEM((features // 16, nodes), jnp.int32),
            pltpu.VMEM((1, row_tiles * col_tiles), jnp.int32),
            pltpu.SMEM((1, row_tiles * col_tiles), jnp.int32),
            pltpu.VMEM((PARTS, part, nodes), BF16),
            pltpu.VMEM((features, features), F32),
            dma((7,)),
            pltpu.VMEM((slots + 1, TILE, TILE), BF16),
            pltpu.VMEM((cols, PARTS, part, nodes), BF16),
            pltpu.VMEM((PARTS, col_tiles // 2, part, PAIR), F32),
            pltpu.VMEM((PARTS, chips, part, nodes), BF16),
            pltpu.VMEM((PARTS, chips, part, nodes), BF16),
            pltpu.VMEM((2, chips, PARTS, part, nodes), BF16),
            pltpu.VMEM((2, chips, PARTS, part, nodes), BF16),
            pltpu.VMEM((features, nodes), F32),
            dma((8,)),
            dma((cols, PARTS)),
            dma((cols, PARTS)),
            dma((PARTS, chips)),
            dma((PARTS, chips)),
            dma((2, chips, PARTS)),
            dma((2, chips, PARTS)),
        ],
        compiler_params=pltpu.CompilerParams(
            collective_id=0, has_side_effects=True, vmem_limit_bytes=56 * 2**20
        ),
        cost_estimate=pl.CostEstimate(
            flops=2 * row_tiles * col_tiles * TILE * TILE * features,
            bytes_accessed=slots * TILE * TILE * 2, transcendentals=0,
        ),
        name="exchange",
    )(out_grad, out_bits.T, agg_saved, weight, tiles[0, 0], tile_coords[0, 0].T, tile_count, in_bits.T)
    hbm_out = pl.BlockSpec(memory_space=pl.ANY)
    prev_grad, weight_grad = pl.pallas_call(
        deliver_all,
        out_shape=(
            jax.ShapeDtypeStruct((nodes, features), BF16),
            jax.ShapeDtypeStruct((features, features), F32),
        ),
        in_specs=[hbm_out] * 2,
        out_specs=(hbm_out, hbm_out),
        scratch_shapes=[
            pltpu.VMEM((nodes, features), BF16),
            pltpu.VMEM((features, features), F32),
            dma((2, 2, 4)),
        ],
        compiler_params=pltpu.CompilerParams(vmem_limit_bytes=56 * 2**20),
        name="deliver",
    )(prev_grad, weight_grad)
    return weight_grad, prev_grad


def solution(mesh):
    return jax.shard_map(
        shards,
        mesh=mesh,
        in_specs=(
            P(("row", "col"), None),
            P(("row", "col"), None),
            P(("row", "col"), None),
            P(),
            P("row", "col", None, None, None),
            P("row", "col", None, None),
            P("row", "col"),
            P(("row", "col"), None),
        ),
        out_specs=(P(), P(("row", "col"), None)),
        check_vma=False,
    )
```

```python
import functools
import math

import jax
import jax.numpy as jnp
from jax import lax
from jax.experimental import pallas as pl
from jax.experimental.pallas import tpu as pltpu
from jax.sharding import PartitionSpec as P

TILE = 128
PAIR = 2 * TILE
PARTS = 2
MESH = pl.DeviceIdType.MESH
F32 = jnp.float32
BF16 = jnp.bfloat16


def bit_mask(bits, features, across):
    words, nodes = bits.shape
    low = (bits & 255).astype(F32).astype(BF16)
    high = ((bits >> 8) & 255).astype(F32).astype(BF16)
    feature = lax.broadcasted_iota(jnp.int32, (words, features), 1)
    word = lax.broadcasted_iota(jnp.int32, (words, features), 0)
    own = (feature >> 4) == word
    in_low = (feature & 15) < 8
    pick_low = jnp.where(own & in_low, 1.0, 0.0).astype(BF16)
    pick_high = jnp.where(own & ~in_low, 1.0, 0.0).astype(BF16)

    def place(pick, byte):
        left, right = (pick, byte) if across else (byte, pick)
        return lax.dot_general(left, right, (((0,), (0,)), ((), ())), preferred_element_type=F32)

    byte = place(pick_low, low) + place(pick_high, high)
    shift = lax.broadcasted_iota(jnp.int32, byte.shape, 0 if across else 1) & 7
    return (byte.astype(jnp.int32) >> shift) & 1


def flip_bits(index, bits, total):
    result = index
    step = 1
    while step < total:
        if bits & step:
            result = result + step * (1 - 2 * ((index // step) % 2))
        step *= 2
    return result


def exchange(
    rows, cols, scale, grad_hbm, bits_hbm, agg_hbm, weight_hbm, tiles_ref, coords_hbm, count_ref, inbits_hbm,
    out_ref, weight_ref,
    by_col, col_sum, by_row, row_sum, col_total, total_buf,
    w1_send, w1_recv, w2_send, w2_recv, w3_send, w3_recv, w4_send, w4_recv,
    grad_buf, bits_buf, agg_buf, mat_buf, coords_buf, inbits_buf, table_buf, table_ref, hidden_ref, part_ref, part_low, load_sem,
    tile_buf, gathered, acc, pair_out, pair_in, chain_out, chain_in, mask_buf,
    tile_sem, hid_send, hid_recv, pair_send, pair_recv, chain_send, chain_recv,
):
    slots = tiles_ref.shape[0]
    nodes, features = grad_hbm.shape
    row_tiles = nodes // TILE
    col_tiles = rows * nodes // TILE
    positions = cols * row_tiles * col_tiles
    pairs_per = nodes // PAIR
    part = features // PARTS
    chips = rows // 2
    my_row = lax.axis_index("row")
    my_col = lax.axis_index("col")
    place = my_row // 2
    core = my_row % 2
    partner = place * 2 + 1 - core

    barrier = pltpu.get_barrier_semaphore()
    peers = [flip_bits(my_col, k, cols) for k in range(cols)]
    mates = [(my_row + i) % rows for i in range(rows)]
    for k in range(1, cols):
        pl.semaphore_signal(barrier, inc=1, device_id=(my_row, peers[k]), device_id_type=MESH)
    for i in range(1, rows):
        pl.semaphore_signal(barrier, inc=1, device_id=(mates[i], my_col), device_id_type=MESH)

    pairs_in = [
        (bits_hbm, bits_buf), (grad_hbm, grad_buf), (weight_hbm, mat_buf),
        (coords_hbm, coords_buf), (inbits_hbm, inbits_buf), (agg_hbm, agg_buf),
    ]
    inputs = [pltpu.make_async_copy(src, dst, load_sem.at[i]) for i, (src, dst) in enumerate(pairs_in)]
    for load in inputs:
        load.start()
    loads = []
    chunk = slots // 8
    for piece in range(8):
        span = pl.ds(piece * chunk, chunk)
        load = pltpu.make_async_copy(tiles_ref.at[span], tile_buf.at[span], tile_sem.at[piece])
        load.start()
        loads.append(load)

    for load in inputs[:3]:
        load.wait()
    mask = bit_mask(bits_buf[...], features, False)
    masked = jnp.where(mask == 1, grad_buf[...].astype(F32), 0.0).astype(BF16)
    hidden_ref[...] = lax.dot_general(
        mat_buf[...], masked, (((1,), (1,)), ((), ())), preferred_element_type=F32
    ).astype(BF16).reshape(PARTS, part, nodes)
    pl.semaphore_wait(barrier, rows + cols - 2)

    def hid_copy(k, p):
        return pltpu.make_async_remote_copy(
            src_ref=hidden_ref.at[p], dst_ref=gathered.at[my_col, p],
            send_sem=hid_send.at[k, p], recv_sem=hid_recv.at[my_col, p],
            device_id=(my_row, peers[k]), device_id_type=MESH,
        )

    def landed(ref, sem):
        pltpu.make_async_copy(ref, ref, sem).wait()

    near = range(1, cols - 1)
    far = range(cols - 1, cols)

    def send(group, p):
        for k in group:
            hid_copy(k, p).start()

    def sent(group, p):
        for k in group:
            hid_copy(k, p).wait_send()

    send(near, 0)
    tile_buf[slots] = jnp.zeros((TILE, TILE), BF16)
    for load in inputs[3:]:
        load.wait()
    spot_of = coords_buf[0:1, :] * col_tiles + coords_buf[1:2, :]
    alive = lax.broadcasted_iota(jnp.int32, (1, slots), 1) < count_ref[0, 0]
    spot_of = jnp.where(alive, spot_of, -1)
    spot_of = jnp.broadcast_to(spot_of, (8, slots)).T[:, 0:1]
    wide = min(512, positions)
    for first in range(0, positions, wide):
        spots = lax.broadcasted_iota(jnp.int32, (slots, wide), 1) + first
        slot = lax.broadcasted_iota(jnp.int32, (slots, wide), 0)
        found = jnp.min(jnp.where(spot_of == spots, slot, slots), axis=0, keepdims=True)
        table_buf[:, first:first + wide] = jnp.minimum(jnp.maximum(found, 0), slots)
    to_scalars = pltpu.make_async_copy(table_buf, table_ref, load_sem.at[len(inputs)])
    to_scalars.start()
    part_ref[...] = scale * lax.dot_general(
        agg_buf[...], masked, (((0,), (0,)), ((), ())), preferred_element_type=F32
    )
    part_low[...] = part_ref[...].astype(BF16)
    mask_buf[...] = bit_mask(inbits_buf[...], features, True).astype(F32)
    sent(near, 0)
    send(far, 0)
    to_scalars.wait()
    for load in loads:
        load.wait()

    def product(source, pair, p=None):
        strips = []
        for i in range(row_tiles):
            base = (source * row_tiles + i) * col_tiles + 2 * pair
            strips.append(
                jnp.concatenate([tile_buf[table_ref[0, base]], tile_buf[table_ref[0, base + 1]]], axis=1)
            )
        left = hidden_ref[...].reshape(features, nodes) if p is None else gathered[source, p]
        return jnp.dot(left, jnp.concatenate(strips, axis=0), preferred_element_type=F32)

    def own_source():
        @pl.loop(0, col_tiles // 2, unroll=4)
        def _(pair):
            value = product(my_col, pair)
            for p in range(PARTS):
                acc[p, pair] = value[p * part:(p + 1) * part]

    def add_sources(group, p):
        for k in group:
            landed(gathered.at[peers[k], p], hid_recv.at[peers[k], p])

        @pl.loop(0, col_tiles // 2, unroll=4)
        def _(pair):
            value = product(peers[group[0]], pair, p)
            for k in group[1:]:
                value += product(peers[k], pair, p)
            acc[p, pair] += value

    band = features // cols
    owners = min(rows, band // 8)
    strip = band // owners

    def w1_copy(k):
        return pltpu.make_async_remote_copy(
            src_ref=part_low.at[pl.ds(pl.multiple_of(peers[k] * band, 16), band)], dst_ref=by_col.at[my_col],
            send_sem=w1_send.at[k], recv_sem=w1_recv.at[my_col],
            device_id=(my_row, peers[k]), device_id_type=MESH,
        )

    def w2_copy(i):
        return pltpu.make_async_remote_copy(
            src_ref=col_sum.at[pl.ds(pl.multiple_of(mates[i] * strip, 8), strip)], dst_ref=by_row.at[my_row],
            send_sem=w2_send.at[i], recv_sem=w2_recv.at[my_row],
            device_id=(mates[i], my_col), device_id_type=MESH,
        )

    def w3_copy(i):
        return pltpu.make_async_remote_copy(
            src_ref=row_sum, dst_ref=col_total.at[pl.ds(pl.multiple_of(my_row * strip, 8), strip)],
            send_sem=w3_send.at[i], recv_sem=w3_recv.at[my_row],
            device_id=(mates[i], my_col), device_id_type=MESH,
        )

    def w4_copy(k):
        return pltpu.make_async_remote_copy(
            src_ref=col_total, dst_ref=total_buf.at[pl.ds(pl.multiple_of(my_col * band, 8), band)],
            send_sem=w4_send.at[k], recv_sem=w4_recv.at[my_col],
            device_id=(my_row, peers[k]), device_id_type=MESH,
        )

    def weight_one():
        for k in range(1, cols):
            w1_copy(k).start()

    def weight_two():
        total = part_ref[pl.ds(pl.multiple_of(my_col * band, 8), band), :]
        for k in range(1, cols):
            landed(by_col.at[peers[k]], w1_recv.at[peers[k]])
            total += by_col[peers[k]].astype(F32)
        col_sum[...] = total
        for i in range(1, rows):
            @pl.when(mates[i] < owners)
            def _():
                w2_copy(i).start()

    def weight_three():
        @pl.when(my_row < owners)
        def _():
            mine = pl.ds(pl.multiple_of(my_row * strip, 8), strip)
            total = col_sum[mine, :]
            for i in range(1, rows):
                landed(by_row.at[mates[i]], w2_recv.at[mates[i]])
                total += by_row[mates[i]]
            row_sum[...] = total
            col_total[mine, :] = total
            for i in range(1, rows):
                w3_copy(i).start()

    def weight_four():
        for i in range(1, rows):
            @pl.when(mates[i] < owners)
            def _():
                landed(col_total.at[pl.ds(pl.multiple_of(mates[i] * strip, 8), strip)], w3_recv.at[mates[i]])
        total_buf[pl.ds(pl.multiple_of(my_col * band, 8), band), :] = col_total[...]
        for k in range(1, cols):
            w4_copy(k).start()

    def weight_end():
        for k in range(1, cols):
            landed(total_buf.at[pl.ds(pl.multiple_of(peers[k] * band, 8), band)], w4_recv.at[peers[k]])
        weight_ref[...] = total_buf[...]
        for k in range(1, cols):
            w1_copy(k).wait_send()
            w4_copy(k).wait_send()
        for i in range(1, rows):
            @pl.when(mates[i] < owners)
            def _():
                w2_copy(i).wait_send()

            @pl.when(my_row < owners)
            def _():
                w3_copy(i).wait_send()

    order = []
    for d in range((chips + 1) // 2):
        order += [chips - 1 - d] + ([d] if d != chips - 1 - d else [])
    way = place // ((chips + 1) // 2)

    def pair_copy(spot, p):
        return pltpu.make_async_remote_copy(
            src_ref=pair_out.at[p, spot], dst_ref=pair_in.at[p, spot],
            send_sem=pair_send.at[p, spot], recv_sem=pair_recv.at[p, spot],
            device_id=(partner, my_col), device_id_type=MESH,
        )

    def finish(p):
        landed(gathered.at[peers[cols - 1], p], hid_recv.at[peers[cols - 1], p])
        for spot in order:
            for j in range(pairs_per):
                pair = (2 * spot + 1 - core) * pairs_per + j
                value = acc[p, pair] + product(peers[cols - 1], pair, p)
                pair_out[p, spot, :, pl.ds(j * PAIR, PAIR)] = value.astype(BF16)
            pair_copy(spot, p).start()
        for spot in order:
            for j in range(pairs_per):
                pair = (2 * spot + core) * pairs_per + j
                acc[p, pair] += product(peers[cols - 1], pair, p)

    def chain_copy(way, spot, p):
        return pltpu.make_async_remote_copy(
            src_ref=chain_out.at[way, spot, p], dst_ref=chain_in.at[way, spot, p],
            send_sem=chain_send.at[way, spot, p], recv_sem=chain_recv.at[way, spot, p],
            device_id=(my_row + 2 - 4 * way, my_col), device_id_type=MESH,
        )

    def local_sum(spot, p):
        first = (2 * spot + core) * pairs_per
        own = jnp.concatenate([acc[p, first + j] for j in range(pairs_per)], axis=1)
        return own + pair_in[p, spot].astype(F32)

    def hop(way, d, p, edge):
        spot = (1 - way) * (chips - 1 - d) + way * d
        ahead = (1 - 2 * way) * (spot - place)
        behind = (1 - way) * place + way * (chips - 1 - place)
        if edge:
            @pl.when((ahead > 0) & (behind == 0))
            def _():
                pair_copy(spot, p).wait_recv()
                chain_out[way, spot, p] = local_sum(spot, p).astype(BF16)
                chain_copy(way, spot, p).start()
        else:
            @pl.when((ahead > 0) & (behind > 0))
            def _():
                pair_copy(spot, p).wait_recv()
                chain_copy(way, spot, p).wait_recv()
                total = local_sum(spot, p) + chain_in[way, spot, p].astype(F32)
                chain_out[way, spot, p] = total.astype(BF16)
                chain_copy(way, spot, p).start()

    def edge_hops(p):
        for d in range(chips - 1):
            hop(0, d, p, True)
            hop(1, d, p, True)

    def middle_hops(p):
        for d in range(chips - 1):
            if d or p:
                hop(way, d, p, False)
            hop(1 - way, d, p, False)

    def deliver(p):
        first = (2 * place + core) * pairs_per
        acc_at = [acc.at[p, first + j] for j in range(pairs_per)]
        pair_copy(place, p).wait_recv()
        for j in range(pairs_per):
            acc_at[j][...] += pair_in[p, place, :, pl.ds(j * PAIR, PAIR)].astype(F32)

        @pl.when(place > 0)
        def _():
            chain_copy(0, place, p).wait_recv()
            for j in range(pairs_per):
                acc_at[j][...] += chain_in[0, place, p, :, pl.ds(j * PAIR, PAIR)].astype(F32)

        @pl.when(place < chips - 1)
        def _():
            chain_copy(1, place, p).wait_recv()
            for j in range(pairs_per):
                acc_at[j][...] += chain_in[1, place, p, :, pl.ds(j * PAIR, PAIR)].astype(F32)

        rows_p = pl.ds(p * part, part)
        for j in range(pairs_per):
            span = pl.ds(j * PAIR, PAIR)
            out_ref[span, rows_p] = jnp.where(mask_buf[rows_p, span] > 0.5, acc_at[j][...], 0.0).T.astype(BF16)

    weight_one()
    own_source()
    sent(far, 0)
    send(near, 1)
    add_sources(near, 0)
    weight_two()
    finish(0)
    weight_three()
    sent(near, 1)
    send(far, 1)
    edge_hops(0)
    add_sources(near, 1)
    weight_four()
    hop(way, 0, 0, False)
    finish(1)
    edge_hops(1)
    middle_hops(0)
    middle_hops(1)
    for p in range(PARTS):
        deliver(p)
    weight_end()
    sent(far, 1)
    for spot in range(chips):
        for p in range(PARTS):
            pair_copy(spot, p).wait_send()

            @pl.when(spot > place)
            def _():
                chain_copy(0, spot, p).wait_send()

            @pl.when(spot < place)
            def _():
                chain_copy(1, spot, p).wait_send()


def deliver_all(prev_in, weight_in, prev_out, weight_out, prev_buf, weight_buf, sems):
    inward, outward = [], []
    for i, (src, buf, dst) in enumerate(((prev_in, prev_buf, prev_out), (weight_in, weight_buf, weight_out))):
        chunk = src.shape[0] // 4
        for j in range(4):
            span = pl.ds(j * chunk, chunk)
            inward.append(pltpu.make_async_copy(src.at[span], buf.at[span], sems.at[0, i, j]))
            outward.append(pltpu.make_async_copy(buf.at[span], dst.at[span], sems.at[1, i, j]))
    for copy in inward:
        copy.start()
    for first, second in zip(inward, outward):
        first.wait()
        second.start()
    for copy in outward:
        copy.wait()


def shards(out_grad, out_bits, agg_saved, weight, tiles, tile_coords, tile_count, in_bits):
    rows = lax.axis_size("row")
    cols = lax.axis_size("col")
    nodes, features = out_grad.shape
    scale = 1.0 / math.sqrt(nodes * rows * cols)
    slots = tiles.shape[2]
    row_tiles = cols * nodes // TILE
    col_tiles = rows * nodes // TILE
    chips = rows // 2
    part = features // PARTS
    vmem = pl.BlockSpec(memory_space=pltpu.VMEM)
    hbm = pl.BlockSpec(memory_space=pltpu.HBM)

    dma = pltpu.SemaphoreType.DMA
    band = features // cols
    strip = band // min(rows, band // 8)
    prev_grad, weight_grad = pl.pallas_call(
        functools.partial(exchange, rows, cols, scale),
        out_shape=(
            jax.ShapeDtypeStruct((nodes, features), BF16),
            jax.ShapeDtypeStruct((features, features), F32),
        ),
        in_specs=[hbm] * 6 + [pl.BlockSpec(memory_space=pltpu.SMEM), hbm],
        out_specs=(vmem, vmem),
        scratch_shapes=[
            pltpu.VMEM((cols, band, features), BF16),
            pltpu.VMEM((band, features), F32),
            pltpu.VMEM((rows, strip, features), F32),
            pltpu.VMEM((strip, features), F32),
            pltpu.VMEM((band, features), F32),
            pltpu.VMEM((features, features), F32),
            dma((cols,)),
            dma((cols,)),
            dma((rows,)),
            dma((rows,)),
            dma((rows,)),
            dma((rows,)),
            dma((cols,)),
            dma((cols,)),
            pltpu.VMEM((nodes, features), BF16),
            pltpu.VMEM((features // 16, nodes), jnp.int32),
            pltpu.VMEM((nodes, features), BF16),
            pltpu.VMEM((features, features), BF16),
            pltpu.VMEM((2, slots), jnp.int32),
            pltpu.VMEM((features // 16, nodes), jnp.int32),
            pltpu.VMEM((1, row_tiles * col_tiles), jnp.int32),
            pltpu.SMEM((1, row_tiles * col_tiles), jnp.int32),
            pltpu.VMEM((PARTS, part, nodes), BF16),
            pltpu.VMEM((features, features), F32),
            pltpu.VMEM((features, features), BF16),
            dma((7,)),
            pltpu.VMEM((slots + 1, TILE, TILE), BF16),
            pltpu.VMEM((cols, PARTS, part, nodes), BF16),
            pltpu.VMEM((PARTS, col_tiles // 2, part, PAIR), F32),
            pltpu.VMEM((PARTS, chips, part, nodes), BF16),
            pltpu.VMEM((PARTS, chips, part, nodes), BF16),
            pltpu.VMEM((2, chips, PARTS, part, nodes), BF16),
            pltpu.VMEM((2, chips, PARTS, part, nodes), BF16),
            pltpu.VMEM((features, nodes), F32),
            dma((8,)),
            dma((cols, PARTS)),
            dma((cols, PARTS)),
            dma((PARTS, chips)),
            dma((PARTS, chips)),
            dma((2, chips, PARTS)),
            dma((2, chips, PARTS)),
        ],
        compiler_params=pltpu.CompilerParams(
            collective_id=0, has_side_effects=True, vmem_limit_bytes=56 * 2**20
        ),
        cost_estimate=pl.CostEstimate(
            flops=2 * row_tiles * col_tiles * TILE * TILE * features,
            bytes_accessed=slots * TILE * TILE * 2, transcendentals=0,
        ),
        name="exchange",
    )(out_grad, out_bits.T, agg_saved, weight, tiles[0, 0], tile_coords[0, 0].T, tile_count, in_bits.T)
    hbm_out = pl.BlockSpec(memory_space=pl.ANY)
    prev_grad, weight_grad = pl.pallas_call(
        deliver_all,
        out_shape=(
            jax.ShapeDtypeStruct((nodes, features), BF16),
            jax.ShapeDtypeStruct((features, features), F32),
        ),
        in_specs=[hbm_out] * 2,
        out_specs=(hbm_out, hbm_out),
        scratch_shapes=[
            pltpu.VMEM((nodes, features), BF16),
            pltpu.VMEM((features, features), F32),
            dma((2, 2, 4)),
        ],
        compiler_params=pltpu.CompilerParams(vmem_limit_bytes=56 * 2**20),
        name="deliver",
    )(prev_grad, weight_grad)
    return weight_grad, prev_grad


def solution(mesh):
    return jax.shard_map(
        shards,
        mesh=mesh,
        in_specs=(
            P(("row", "col"), None),
            P(("row", "col"), None),
            P(("row", "col"), None),
            P(),
            P("row", "col", None, None, None),
            P("row", "col", None, None),
            P("row", "col"),
            P(("row", "col"), None),
        ),
        out_specs=(P(), P(("row", "col"), None)),
        check_vma=False,
    )
```

```python
import functools
import math

import jax
import jax.numpy as jnp
from jax import lax
from jax.experimental import pallas as pl
from jax.experimental.pallas import tpu as pltpu
from jax.sharding import PartitionSpec as P

TILE = 128
PAIR = 2 * TILE
PARTS = 2
MESH = pl.DeviceIdType.MESH
F32 = jnp.float32
BF16 = jnp.bfloat16


def bit_mask(bits, features, across):
    words, nodes = bits.shape
    low = (bits & 255).astype(F32).astype(BF16)
    high = ((bits >> 8) & 255).astype(F32).astype(BF16)
    feature = lax.broadcasted_iota(jnp.int32, (words, features), 1)
    word = lax.broadcasted_iota(jnp.int32, (words, features), 0)
    own = (feature >> 4) == word
    in_low = (feature & 15) < 8
    pick_low = jnp.where(own & in_low, 1.0, 0.0).astype(BF16)
    pick_high = jnp.where(own & ~in_low, 1.0, 0.0).astype(BF16)

    def place(pick, byte):
        left, right = (pick, byte) if across else (byte, pick)
        return lax.dot_general(left, right, (((0,), (0,)), ((), ())), preferred_element_type=F32)

    byte = place(pick_low, low) + place(pick_high, high)
    shift = lax.broadcasted_iota(jnp.int32, byte.shape, 0 if across else 1) & 7
    return (byte.astype(jnp.int32) >> shift) & 1


def flip_bits(index, bits, total):
    result = index
    step = 1
    while step < total:
        if bits & step:
            result = result + step * (1 - 2 * ((index // step) % 2))
        step *= 2
    return result


def exchange(
    rows, cols, scale, grad_hbm, bits_hbm, agg_hbm, weight_hbm, tiles_ref, coords_hbm, count_ref, inbits_hbm,
    out_ref, weight_ref,
    by_col, col_sum, by_row, row_sum, col_total, total_buf,
    w1_send, w1_recv, w2_send, w2_recv, w3_send, w3_recv, w4_send, w4_recv,
    grad_buf, bits_buf, agg_buf, mat_buf, coords_buf, inbits_buf, table_buf, table_ref, hidden_ref, part_ref, part_low, load_sem,
    tile_buf, gathered, acc, pair_out, pair_in, chain_out, chain_in, mask_buf,
    tile_sem, hid_send, hid_recv, pair_send, pair_recv, chain_send, chain_recv,
):
    slots = tiles_ref.shape[0]
    nodes, features = grad_hbm.shape
    row_tiles = nodes // TILE
    col_tiles = rows * nodes // TILE
    positions = cols * row_tiles * col_tiles
    pairs_per = nodes // PAIR
    part = features // PARTS
    chips = rows // 2
    my_row = lax.axis_index("row")
    my_col = lax.axis_index("col")
    place = my_row // 2
    core = my_row % 2
    partner = place * 2 + 1 - core

    barrier = pltpu.get_barrier_semaphore()
    peers = [flip_bits(my_col, k, cols) for k in range(cols)]
    mates = [(my_row + i) % rows for i in range(rows)]
    for k in range(1, cols):
        pl.semaphore_signal(barrier, inc=1, device_id=(my_row, peers[k]), device_id_type=MESH)
    for i in range(1, rows):
        pl.semaphore_signal(barrier, inc=1, device_id=(mates[i], my_col), device_id_type=MESH)

    pairs_in = [
        (bits_hbm, bits_buf), (grad_hbm, grad_buf), (weight_hbm, mat_buf),
        (coords_hbm, coords_buf), (inbits_hbm, inbits_buf), (agg_hbm, agg_buf),
    ]
    inputs = [pltpu.make_async_copy(src, dst, load_sem.at[i]) for i, (src, dst) in enumerate(pairs_in)]
    for load in inputs:
        load.start()
    loads = []
    chunk = slots // 8
    for piece in range(8):
        span = pl.ds(piece * chunk, chunk)
        load = pltpu.make_async_copy(tiles_ref.at[span], tile_buf.at[span], tile_sem.at[piece])
        load.start()
        loads.append(load)

    for load in inputs[:3]:
        load.wait()
    mask = bit_mask(bits_buf[...], features, False)
    masked = jnp.where(mask == 1, grad_buf[...].astype(F32), 0.0).astype(BF16)
    hidden_ref[...] = lax.dot_general(
        mat_buf[...], masked, (((1,), (1,)), ((), ())), preferred_element_type=F32
    ).astype(BF16).reshape(PARTS, part, nodes)
    pl.semaphore_wait(barrier, rows + cols - 2)

    def hid_copy(k, p):
        return pltpu.make_async_remote_copy(
            src_ref=hidden_ref.at[p], dst_ref=gathered.at[my_col, p],
            send_sem=hid_send.at[k, p], recv_sem=hid_recv.at[my_col, p],
            device_id=(my_row, peers[k]), device_id_type=MESH,
        )

    def landed(ref, sem):
        pltpu.make_async_copy(ref, ref, sem).wait()

    near = range(1, cols - 1)
    far = range(cols - 1, cols)

    def send(group, p):
        for k in group:
            hid_copy(k, p).start()

    def sent(group, p):
        for k in group:
            hid_copy(k, p).wait_send()

    send(near, 0)
    tile_buf[slots] = jnp.zeros((TILE, TILE), BF16)
    for load in inputs[3:]:
        load.wait()
    spot_of = coords_buf[0:1, :] * col_tiles + coords_buf[1:2, :]
    alive = lax.broadcasted_iota(jnp.int32, (1, slots), 1) < count_ref[0, 0]
    spot_of = jnp.where(alive, spot_of, -1)
    spot_of = jnp.broadcast_to(spot_of, (8, slots)).T[:, 0:1]
    wide = min(512, positions)
    for first in range(0, positions, wide):
        spots = lax.broadcasted_iota(jnp.int32, (slots, wide), 1) + first
        slot = lax.broadcasted_iota(jnp.int32, (slots, wide), 0)
        found = jnp.min(jnp.where(spot_of == spots, slot, slots), axis=0, keepdims=True)
        table_buf[:, first:first + wide] = jnp.minimum(jnp.maximum(found, 0), slots)
    to_scalars = pltpu.make_async_copy(table_buf, table_ref, load_sem.at[len(inputs)])
    to_scalars.start()
    part_ref[...] = scale * lax.dot_general(
        agg_buf[...], masked, (((0,), (0,)), ((), ())), preferred_element_type=F32
    )
    part_low[...] = part_ref[...].astype(BF16)
    mask_buf[...] = bit_mask(inbits_buf[...], features, True).astype(F32)
    sent(near, 0)
    send(far, 0)
    to_scalars.wait()
    for load in loads:
        load.wait()

    def product(source, pair, p=None):
        strips = []
        for i in range(row_tiles):
            base = (source * row_tiles + i) * col_tiles + 2 * pair
            strips.append(
                jnp.concatenate([tile_buf[table_ref[0, base]], tile_buf[table_ref[0, base + 1]]], axis=1)
            )
        left = hidden_ref[...].reshape(features, nodes) if p is None else gathered[source, p]
        return jnp.dot(left, jnp.concatenate(strips, axis=0), preferred_element_type=F32)

    def own_source():
        @pl.loop(0, col_tiles // 2, unroll=4)
        def _(pair):
            value = product(my_col, pair)
            for p in range(PARTS):
                acc[p, pair] = value[p * part:(p + 1) * part]

    def add_sources(group, p):
        for k in group:
            landed(gathered.at[peers[k], p], hid_recv.at[peers[k], p])

        @pl.loop(0, col_tiles // 2, unroll=4)
        def _(pair):
            value = product(peers[group[0]], pair, p)
            for k in group[1:]:
                value += product(peers[k], pair, p)
            acc[p, pair] += value

    band = features // cols
    owners = min(rows, band // 8)
    strip = band // owners

    def w1_copy(k):
        return pltpu.make_async_remote_copy(
            src_ref=part_low.at[pl.ds(pl.multiple_of(peers[k] * band, 16), band)], dst_ref=by_col.at[my_col],
            send_sem=w1_send.at[k], recv_sem=w1_recv.at[my_col],
            device_id=(my_row, peers[k]), device_id_type=MESH,
        )

    def w2_copy(i):
        return pltpu.make_async_remote_copy(
            src_ref=col_sum.at[pl.ds(pl.multiple_of(mates[i] * strip, 8), strip)], dst_ref=by_row.at[my_row],
            send_sem=w2_send.at[i], recv_sem=w2_recv.at[my_row],
            device_id=(mates[i], my_col), device_id_type=MESH,
        )

    def w3_copy(i):
        return pltpu.make_async_remote_copy(
            src_ref=row_sum, dst_ref=col_total.at[pl.ds(pl.multiple_of(my_row * strip, 8), strip)],
            send_sem=w3_send.at[i], recv_sem=w3_recv.at[my_row],
            device_id=(mates[i], my_col), device_id_type=MESH,
        )

    def w4_copy(k):
        return pltpu.make_async_remote_copy(
            src_ref=col_total, dst_ref=total_buf.at[pl.ds(pl.multiple_of(my_col * band, 8), band)],
            send_sem=w4_send.at[k], recv_sem=w4_recv.at[my_col],
            device_id=(my_row, peers[k]), device_id_type=MESH,
        )

    def weight_one():
        for k in range(1, cols):
            w1_copy(k).start()

    def weight_two():
        total = part_ref[pl.ds(pl.multiple_of(my_col * band, 8), band), :]
        for k in range(1, cols):
            landed(by_col.at[peers[k]], w1_recv.at[peers[k]])
            total += by_col[peers[k]].astype(F32)
        col_sum[...] = total
        for i in range(1, rows):
            @pl.when(mates[i] < owners)
            def _():
                w2_copy(i).start()

    def weight_three():
        @pl.when(my_row < owners)
        def _():
            mine = pl.ds(pl.multiple_of(my_row * strip, 8), strip)
            total = col_sum[mine, :]
            for i in range(1, rows):
                landed(by_row.at[mates[i]], w2_recv.at[mates[i]])
                total += by_row[mates[i]]
            row_sum[...] = total
            col_total[mine, :] = total
            for i in range(1, rows):
                w3_copy(i).start()

    def weight_four():
        for i in range(1, rows):
            @pl.when(mates[i] < owners)
            def _():
                landed(col_total.at[pl.ds(pl.multiple_of(mates[i] * strip, 8), strip)], w3_recv.at[mates[i]])
        total_buf[pl.ds(pl.multiple_of(my_col * band, 8), band), :] = col_total[...]
        for k in range(1, cols):
            w4_copy(k).start()

    def weight_end():
        for k in range(1, cols):
            landed(total_buf.at[pl.ds(pl.multiple_of(peers[k] * band, 8), band)], w4_recv.at[peers[k]])
        weight_ref[...] = total_buf[...]
        for k in range(1, cols):
            w1_copy(k).wait_send()
            w4_copy(k).wait_send()
        for i in range(1, rows):
            @pl.when(mates[i] < owners)
            def _():
                w2_copy(i).wait_send()

            @pl.when(my_row < owners)
            def _():
                w3_copy(i).wait_send()

    order = []
    for d in range((chips + 1) // 2):
        order += [chips - 1 - d] + ([d] if d != chips - 1 - d else [])
    way = place // ((chips + 1) // 2)

    def pair_copy(spot, p):
        return pltpu.make_async_remote_copy(
            src_ref=pair_out.at[p, spot], dst_ref=pair_in.at[p, spot],
            send_sem=pair_send.at[p, spot], recv_sem=pair_recv.at[p, spot],
            device_id=(partner, my_col), device_id_type=MESH,
        )

    def finish(p):
        landed(gathered.at[peers[cols - 1], p], hid_recv.at[peers[cols - 1], p])
        for spot in order:
            for j in range(pairs_per):
                pair = (2 * spot + 1 - core) * pairs_per + j
                value = acc[p, pair] + product(peers[cols - 1], pair, p)
                pair_out[p, spot, :, pl.ds(j * PAIR, PAIR)] = value.astype(BF16)
            pair_copy(spot, p).start()
            for j in range(pairs_per):
                pair = (2 * spot + core) * pairs_per + j
                acc[p, pair] += product(peers[cols - 1], pair, p)

    def chain_copy(way, spot, p):
        return pltpu.make_async_remote_copy(
            src_ref=chain_out.at[way, spot, p], dst_ref=chain_in.at[way, spot, p],
            send_sem=chain_send.at[way, spot, p], recv_sem=chain_recv.at[way, spot, p],
            device_id=(my_row + 2 - 4 * way, my_col), device_id_type=MESH,
        )

    def local_sum(spot, p):
        first = (2 * spot + core) * pairs_per
        own = jnp.concatenate([acc[p, first + j] for j in range(pairs_per)], axis=1)
        return own + pair_in[p, spot].astype(F32)

    def hop(way, d, p, edge):
        spot = (1 - way) * (chips - 1 - d) + way * d
        ahead = (1 - 2 * way) * (spot - place)
        behind = (1 - way) * place + way * (chips - 1 - place)
        if edge:
            @pl.when((ahead > 0) & (behind == 0))
            def _():
                pair_copy(spot, p).wait_recv()
                chain_out[way, spot, p] = local_sum(spot, p).astype(BF16)
                chain_copy(way, spot, p).start()
        else:
            @pl.when((ahead > 0) & (behind > 0))
            def _():
                pair_copy(spot, p).wait_recv()
                chain_copy(way, spot, p).wait_recv()
                total = local_sum(spot, p) + chain_in[way, spot, p].astype(F32)
                chain_out[way, spot, p] = total.astype(BF16)
                chain_copy(way, spot, p).start()

    def edge_hops(p):
        for d in range(chips - 1):
            hop(0, d, p, True)
            hop(1, d, p, True)

    def middle_hops(p):
        for d in range(chips - 1):
            if d or p:
                hop(way, d, p, False)
            hop(1 - way, d, p, False)

    def deliver(p):
        first = (2 * place + core) * pairs_per
        acc_at = [acc.at[p, first + j] for j in range(pairs_per)]
        pair_copy(place, p).wait_recv()
        for j in range(pairs_per):
            acc_at[j][...] += pair_in[p, place, :, pl.ds(j * PAIR, PAIR)].astype(F32)

        @pl.when(place > 0)
        def _():
            chain_copy(0, place, p).wait_recv()
            for j in range(pairs_per):
                acc_at[j][...] += chain_in[0, place, p, :, pl.ds(j * PAIR, PAIR)].astype(F32)

        @pl.when(place < chips - 1)
        def _():
            chain_copy(1, place, p).wait_recv()
            for j in range(pairs_per):
                acc_at[j][...] += chain_in[1, place, p, :, pl.ds(j * PAIR, PAIR)].astype(F32)

        rows_p = pl.ds(p * part, part)
        for j in range(pairs_per):
            span = pl.ds(j * PAIR, PAIR)
            out_ref[span, rows_p] = jnp.where(mask_buf[rows_p, span] > 0.5, acc_at[j][...], 0.0).T.astype(BF16)

    weight_one()
    own_source()
    sent(far, 0)
    send(near, 1)
    add_sources(near, 0)
    finish(0)
    sent(near, 1)
    send(far, 1)
    weight_two()
    edge_hops(0)
    add_sources(near, 1)
    weight_three()
    hop(way, 0, 0, False)
    finish(1)
    edge_hops(1)
    middle_hops(0)
    weight_four()
    middle_hops(1)
    for p in range(PARTS):
        deliver(p)
    weight_end()
    sent(far, 1)
    for spot in range(chips):
        for p in range(PARTS):
            pair_copy(spot, p).wait_send()

            @pl.when(spot > place)
            def _():
                chain_copy(0, spot, p).wait_send()

            @pl.when(spot < place)
            def _():
                chain_copy(1, spot, p).wait_send()


def deliver_all(prev_in, weight_in, prev_out, weight_out, prev_buf, weight_buf, sems):
    inward, outward = [], []
    for i, (src, buf, dst) in enumerate(((prev_in, prev_buf, prev_out), (weight_in, weight_buf, weight_out))):
        chunk = src.shape[0] // 4
        for j in range(4):
            span = pl.ds(j * chunk, chunk)
            inward.append(pltpu.make_async_copy(src.at[span], buf.at[span], sems.at[0, i, j]))
            outward.append(pltpu.make_async_copy(buf.at[span], dst.at[span], sems.at[1, i, j]))
    for copy in inward:
        copy.start()
    for first, second in zip(inward, outward):
        first.wait()
        second.start()
    for copy in outward:
        copy.wait()


def shards(out_grad, out_bits, agg_saved, weight, tiles, tile_coords, tile_count, in_bits):
    rows = lax.axis_size("row")
    cols = lax.axis_size("col")
    nodes, features = out_grad.shape
    scale = 1.0 / math.sqrt(nodes * rows * cols)
    slots = tiles.shape[2]
    row_tiles = cols * nodes // TILE
    col_tiles = rows * nodes // TILE
    chips = rows // 2
    part = features // PARTS
    vmem = pl.BlockSpec(memory_space=pltpu.VMEM)
    hbm = pl.BlockSpec(memory_space=pltpu.HBM)

    dma = pltpu.SemaphoreType.DMA
    band = features // cols
    strip = band // min(rows, band // 8)
    prev_grad, weight_grad = pl.pallas_call(
        functools.partial(exchange, rows, cols, scale),
        out_shape=(
            jax.ShapeDtypeStruct((nodes, features), BF16),
            jax.ShapeDtypeStruct((features, features), F32),
        ),
        in_specs=[hbm] * 6 + [pl.BlockSpec(memory_space=pltpu.SMEM), hbm],
        out_specs=(vmem, vmem),
        scratch_shapes=[
            pltpu.VMEM((cols, band, features), BF16),
            pltpu.VMEM((band, features), F32),
            pltpu.VMEM((rows, strip, features), F32),
            pltpu.VMEM((strip, features), F32),
            pltpu.VMEM((band, features), F32),
            pltpu.VMEM((features, features), F32),
            dma((cols,)),
            dma((cols,)),
            dma((rows,)),
            dma((rows,)),
            dma((rows,)),
            dma((rows,)),
            dma((cols,)),
            dma((cols,)),
            pltpu.VMEM((nodes, features), BF16),
            pltpu.VMEM((features // 16, nodes), jnp.int32),
            pltpu.VMEM((nodes, features), BF16),
            pltpu.VMEM((features, features), BF16),
            pltpu.VMEM((2, slots), jnp.int32),
            pltpu.VMEM((features // 16, nodes), jnp.int32),
            pltpu.VMEM((1, row_tiles * col_tiles), jnp.int32),
            pltpu.SMEM((1, row_tiles * col_tiles), jnp.int32),
            pltpu.VMEM((PARTS, part, nodes), BF16),
            pltpu.VMEM((features, features), F32),
            pltpu.VMEM((features, features), BF16),
            dma((7,)),
            pltpu.VMEM((slots + 1, TILE, TILE), BF16),
            pltpu.VMEM((cols, PARTS, part, nodes), BF16),
            pltpu.VMEM((PARTS, col_tiles // 2, part, PAIR), F32),
            pltpu.VMEM((PARTS, chips, part, nodes), BF16),
            pltpu.VMEM((PARTS, chips, part, nodes), BF16),
            pltpu.VMEM((2, chips, PARTS, part, nodes), BF16),
            pltpu.VMEM((2, chips, PARTS, part, nodes), BF16),
            pltpu.VMEM((features, nodes), F32),
            dma((8,)),
            dma((cols, PARTS)),
            dma((cols, PARTS)),
            dma((PARTS, chips)),
            dma((PARTS, chips)),
            dma((2, chips, PARTS)),
            dma((2, chips, PARTS)),
        ],
        compiler_params=pltpu.CompilerParams(
            collective_id=0, has_side_effects=True, vmem_limit_bytes=56 * 2**20
        ),
        cost_estimate=pl.CostEstimate(
            flops=2 * row_tiles * col_tiles * TILE * TILE * features,
            bytes_accessed=slots * TILE * TILE * 2, transcendentals=0,
        ),
        name="exchange",
    )(out_grad, out_bits.T, agg_saved, weight, tiles[0, 0], tile_coords[0, 0].T, tile_count, in_bits.T)
    hbm_out = pl.BlockSpec(memory_space=pl.ANY)
    prev_grad, weight_grad = pl.pallas_call(
        deliver_all,
        out_shape=(
            jax.ShapeDtypeStruct((nodes, features), BF16),
            jax.ShapeDtypeStruct((features, features), F32),
        ),
        in_specs=[hbm_out] * 2,
        out_specs=(hbm_out, hbm_out),
        scratch_shapes=[
            pltpu.VMEM((nodes, features), BF16),
            pltpu.VMEM((features, features), F32),
            dma((2, 2, 4)),
        ],
        compiler_params=pltpu.CompilerParams(vmem_limit_bytes=56 * 2**20),
        name="deliver",
    )(prev_grad, weight_grad)
    return weight_grad, prev_grad


def solution(mesh):
    return jax.shard_map(
        shards,
        mesh=mesh,
        in_specs=(
            P(("row", "col"), None),
            P(("row", "col"), None),
            P(("row", "col"), None),
            P(),
            P("row", "col", None, None, None),
            P("row", "col", None, None),
            P("row", "col"),
            P(("row", "col"), None),
        ),
        out_specs=(P(), P(("row", "col"), None)),
        check_vma=False,
    )
```
